128 devices in a mesh: tm: 32 (over z, y, core), blk: 4 (over x).
Axes of the slice: x: 4, y: 4, z: 4, core: 2. Of those that a mesh axis runs over, the one named last changes fastest.
Arguments:
- filt_mean: float32 [96, 512], P('tm'), may hold values from -6 to 6
- filt_cov: float32 [96, 512, 512], P('tm', 'blk'), may hold values from -1 to 2, as said below
- pred_prec: float32 [96, 512, 512], P('tm', 'blk'), may hold values from -1 to 1.1, as said below
- transition: float32 [512, 512], replicated, may hold values from -1 to 1, as said below
Outputs:
- smooth_mean: float32 [96, 512], P('tm')
- smooth_cov: float32 [96, 512, 512], P('tm', 'blk')
The draws below stay inside these ranges and needn't reach their ends.
Inputs may be any that keep to these rules, and one draw needn't show every extreme that they name: `filt_cov`: each matrix is exactly symmetric, its diagonal between 1 and 2. `pred_prec`: each matrix is exactly symmetric. `transition`: diagonal between 0.985 and 1.
All inputs are finite; a program needn't handle non-finite values.
Results may differ from the reference program's by a relative error of at most 0.0003.
Values sent between devices are 32-bit elements; how exact they have to be, the bound alone decides.
No kernel may reach another device: no remote copies, remote signals or barrier semaphores. Data moves between devices by JAX's collectives and lax.ppermute only.
A program may use at most 256 MiB of HBM per device.

```python
import math
import jax
import jax.numpy as jnp
from jax import lax

STATE = 512
WINDOW_STEPS = 96


def cov_diagonal(key):
    level = jax.random.uniform(jax.random.fold_in(key, 101), (WINDOW_STEPS, STATE), jnp.float32)
    return 2.0 ** level


def transition_diagonal(key):
    level = jax.random.uniform(jax.random.fold_in(key, 102), (STATE,), jnp.float32)
    return 0.985 * (1.0 / 0.985) ** level


def target_gain(key, rate_low, rate_high):
    level = jax.random.uniform(jax.random.fold_in(key, 103), (STATE,), jnp.float32)
    rate_base = rate_low * (rate_high / rate_low) ** level
    jitter = 2.0 ** jax.random.uniform(jax.random.fold_in(key, 104), (WINDOW_STEPS, STATE), jnp.float32, -0.5, 0.5)
    gains = 1.0 - rate_base[None, :] * jitter
    cluster_steps = jax.random.randint(jax.random.fold_in(key, 105), (3,), 0, WINDOW_STEPS)
    cluster_depth = jax.random.uniform(jax.random.fold_in(key, 106), (3,), jnp.float32, 0.5, 0.8)
    match_count = jnp.arange(WINDOW_STEPS)[:, None] == cluster_steps[None, :]
    multiplier = jnp.prod(jnp.where(match_count, cluster_depth[None, :], 1.0), axis=1)
    return gains * multiplier[:, None]


def symmetric_part(key, diagonal, spread, power):
    raw_values = jax.random.uniform(key, (WINDOW_STEPS, STATE, STATE), jnp.float32, -1.0, 1.0)
    raw_values = jnp.sign(raw_values) * jnp.abs(raw_values) ** power
    off_part = (raw_values + jnp.swapaxes(raw_values, 1, 2)) * (0.5 * spread)
    eye_mat = jnp.eye(STATE, dtype=jnp.float32)
    return off_part * (1.0 - eye_mat) + diagonal[:, :, None] * eye_mat


def draw_filt_cov(key, part):
    diagonal = cov_diagonal(key)
    key = jax.random.fold_in(key, 11)
    return symmetric_part(key, diagonal, 0.3 / math.sqrt(STATE), 1.0)


def draw_pred_prec(key, part):
    cov_diag = cov_diagonal(key)
    tran_diag = transition_diagonal(key)
    gains = target_gain(key, 0.02, 0.12)
    key = jax.random.fold_in(key, 23)
    diagonal = gains / (cov_diag * tran_diag[None, :])
    return symmetric_part(key, diagonal, 0.13 / math.sqrt(STATE), 1.0)


def draw_transition(key, part):
    diagonal = transition_diagonal(key)
    key = jax.random.fold_in(key, 37)
    off_part = jax.random.uniform(key, (STATE, STATE), jnp.float32, -1.0, 1.0)
    spread = 0.06 / math.sqrt(STATE)
    eye_mat = jnp.eye(STATE, dtype=jnp.float32)
    return off_part * spread * (1.0 - eye_mat) + diagonal[:, None] * eye_mat


def block_scale(stream_key, extent, split, smallest, high):
    gain = 1.0
    for dim, blocks in split:
        draws = jax.random.uniform(jax.random.fold_in(jax.random.fold_in(stream_key, 6), dim), (blocks,), jnp.float32, smallest / len(split), high / len(split))
        gain = gain * jnp.repeat(jnp.exp(draws), extent[dim] // blocks).reshape((-1,) + (1,) * (len(extent) - 1 - dim))
    return gain


def gaussian(rng, dims, scale, limit, cuts=(), kind=jnp.bfloat16):
    loudness = block_scale(rng, dims, cuts, -0.22, 0.18) if cuts else 1.0
    entries = jax.random.normal(rng, dims, jnp.float32) * scale * loudness
    return jnp.minimum(jnp.maximum(entries, -limit), limit).astype(kind)


def setup_inputs(seed: int = 0) -> dict:
    key_list = jax.random.split(jax.random.key(seed), 5)
    filt_mean = gaussian(key_list[0], (WINDOW_STEPS, STATE), 1.0, 6.0, ((0, 32),), jnp.float32)
    filt_cov = draw_filt_cov(jax.random.fold_in(key_list[4], 71), 0)
    pred_prec = draw_pred_prec(jax.random.fold_in(key_list[4], 71), 0)
    transition = draw_transition(jax.random.fold_in(key_list[4], 71), 0)
    return {"filt_mean": filt_mean, "filt_cov": filt_cov, "pred_prec": pred_prec, "transition": transition}


def matmul(left, right):
    return jnp.matmul(left, right, precision=lax.Precision.HIGHEST)


def reference(filt_mean, filt_cov, pred_prec, transition):
    def backward(carry, inputs):
        mean_following, cov_next = carry
        mean_now, cov_now, prec_now, is_last = inputs
        gain_mat = matmul(matmul(cov_now, transition.T), prec_now)
        offset = mean_now - matmul(gain_mat, matmul(transition, mean_now))
        remainder = cov_now - matmul(gain_mat, matmul(transition, cov_now))
        gain_mat = jnp.where(is_last, jnp.zeros_like(gain_mat), gain_mat)
        offset = jnp.where(is_last, mean_now, offset)
        remainder = jnp.where(is_last, cov_now, remainder)
        mean_new = offset + matmul(gain_mat, mean_following)
        cov_new = matmul(matmul(gain_mat, cov_next), gain_mat.T) + remainder
        return (mean_new, cov_new), (mean_new, cov_new)

    final_flags = jnp.arange(WINDOW_STEPS) == WINDOW_STEPS - 1
    start = (jnp.zeros((STATE,), jnp.float32), jnp.zeros((STATE, STATE), jnp.float32))
    unused, outputs = lax.scan(backward, start, (filt_mean, filt_cov, pred_prec, final_flags), reverse=True)
    return outputs[0], outputs[1]
```

```python
import jax
import jax.numpy as jnp
from jax import lax
from jax.experimental import pallas as pl
from jax.experimental.pallas import tpu as pltpu
from jax.sharding import PartitionSpec as P

N = 512
B = 128
A = 520
F32 = jnp.float32
VM = pl.BlockSpec(memory_space=pltpu.VMEM)
SM = pl.BlockSpec(memory_space=pltpu.SMEM)


def split(v):
    hi = v.astype(jnp.bfloat16)
    return hi, (v - hi.astype(F32)).astype(jnp.bfloat16)


def dot(a, b, nt):
    return lax.dot_general(a, b, (((1,), (1 if nt else 0,)), ((), ())), preferred_element_type=F32)


def mm(a, b, nt=False):
    (ah, al), (bh, bl) = a, b
    return dot(ah, bh, nt) + (dot(ah, bl, nt) + dot(al, bh, nt))


def call(body, outs, args, specs, scratch=(), flops=0, name=None):
    return pl.pallas_call(
        body,
        out_shape=outs,
        in_specs=specs,
        out_specs=jax.tree.map(lambda _: VM, outs),
        scratch_shapes=list(scratch),
        compiler_params=pltpu.CompilerParams(vmem_limit_bytes=40 * 2**20),
        cost_estimate=pl.CostEstimate(flops=flops, bytes_accessed=4 * 2**20, transcendentals=0),
        name=name,
    )(*args)


def sds(*shape):
    return jax.ShapeDtypeStruct(shape, F32)


def assemble(ref, row, known):
    for j in range(4):
        ref[0:B, j * B : (j + 1) * B] = row[:, j * B : (j + 1) * B]
        if j:
            ref[j * B : (j + 1) * B, 0:B] = row[:, j * B : (j + 1) * B].T
    for (i, j), block in known.items():
        ref[i * B : (i + 1) * B, j * B : (j + 1) * B] = block
        if i != j:
            ref[j * B : (j + 1) * B, i * B : (i + 1) * B] = block.T


def step_kernel(first, flag, c, p, fr, fl, c22, p22, t, mean, *rest):
    if first:
        go, ro, cf, pf = rest
    else:
        ga, ra, go, ro, cf, pf = rest
    blk = lambda ref, j: ref[:, j * B : (j + 1) * B]
    assemble(cf, c, {(1, 1): blk(fr, 0), (1, 2): blk(fr, 1), (1, 3): blk(fr, 2),
                     (3, 3): blk(fl, 0), (3, 2): blk(fl, 1), (2, 2): c22[...]})
    cf[N:A, :] = mean[...]
    assemble(pf, p, {(1, 1): blk(fr, 3), (1, 2): blk(fr, 4), (3, 3): blk(fl, 2),
                     (3, 1): blk(fl, 3), (3, 2): blk(fl, 4), (2, 2): p22[...]})
    n = mm(split(cf[...]), split(t[...]), True)
    n = jnp.where(flag[0] == 1, 0.0, n)
    g = mm(split(n[:N]), split(pf[...]))
    gs = split(g)
    if first:
        go[...] = g
        ro[...] = cf[...] - mm(split(n), gs, True)
    else:
        go[...] = mm(gs, split(ga[...]))
        r = ra[...]
        z = mm(gs, split(r[:N]))
        z = jnp.concatenate([z, r[N:]], 0) - n
        ro[...] = cf[...] + mm(split(z), gs, True)


def pair_kernel(core, g, r, go, ro, u):
    @pl.when(core[0] == 0)
    def _():
        u[0:N] = mm(split(g[...]), split(go[...]))
        u[N:A] = jnp.zeros((A - N, N), F32)

    @pl.when(core[0] == 1)
    def _():
        gs = split(go[...])
        z = mm(gs, split(r[0:N]))
        u[...] = ro[...] + mm(split(jnp.concatenate([z, r[N:A]], 0)), gs, True)


def plane_kernel(info, u0, u1, u2, u3, g0, g1, g2, g3, total, suffix, rs, gs):
    core, y = info[0], info[1]
    for d, (ur, gr) in enumerate(((u0, g0), (u1, g1), (u2, g2), (u3, g3))):
        at = lax.rem(y + d, 4)
        rs[at] = ur[...]

        @pl.when(core == 1)
        def _():
            gs[at] = gr[...]

    @pl.when(core == 0)
    def _():
        run = rs[3][:N]
        suffix[N:A] = jnp.zeros((A - N, N), F32)
        eye = (lax.broadcasted_iota(jnp.int32, (N, N), 0) == lax.broadcasted_iota(jnp.int32, (N, N), 1)).astype(F32)
        suffix[0:N] = jnp.where(y == 3, eye, run)
        for i in (2, 1, 0):
            run = mm(split(rs[i][:N]), split(run))
            if i:
                @pl.when(y < i)
                def _():
                    suffix[0:N] = run
        total[0:N] = run
        total[N:A] = jnp.zeros((A - N, N), F32)

    @pl.when(core == 1)
    def _():
        run = rs[3]
        suffix[...] = jnp.where(y == 3, 0.0, run)
        for i in (2, 1, 0):
            g = split(gs[i])
            z = mm(g, split(run[:N]))
            run = rs[i] + mm(split(jnp.concatenate([z, run[N:]], 0)), g, True)
            if i:
                @pl.when(y < i)
                def _():
                    suffix[...] = run
        total[...] = run


def fold_kernel(core, ga, gb, gc, ra, rb, rc, dg, dr, ge, re, oa, ob, oc, sa, sb, sc, tg, tr):
    @pl.when(core[0] == 0)
    def _():
        g = split(ge[...])
        tg[...] = mm(g, split(dg[...]))
        z = mm(g, split(dr[0:N]))
        tr[...] = re[...] + mm(split(jnp.concatenate([z, dr[N:A]], 0)), g, True)

    @pl.when(core[0] == 1)
    def _():
        tg[...] = dg[...]
        tr[...] = dr[...]

    ds = split(tg[...])
    rs = split(tr[0:N])
    for g, r, o, s in ((ga, ra, oa, sa), (gb, rb, ob, sb), (gc, rc, oc, sc)):
        gsp = split(g[...])
        o[...] = mm(gsp, ds)
        z = mm((gsp[0][:B], gsp[1][:B]), rs)
        s[...] = r[...] + mm(split(jnp.concatenate([z, tr[N:A]], 0)), gsp, True)


def final_kernel(info, g1, g2, r1, r2, r3, ga, gb, gc, ra, rb, rc, cov, mean):
    z, x = info[0], info[1]
    run = jnp.where(z + 3 > 3, 0.0, r3[...])
    for d, g, r in ((2, g2, r2), (1, g1, r1)):
        gs = split(g[...])
        zz = mm(gs, split(run[:N]))
        run = jnp.where(z + d > 3, 0.0, r[...]) + mm(split(jnp.concatenate([zz, run[N:]], 0)), gs, True)
    rs = split(run[:N])
    for k, (g, r) in enumerate(((ga, ra), (gb, rb), (gc, rc))):
        gs = split(g[...])
        zz = mm((gs[0][:B], gs[1][:B]), rs)
        out = r[...] + mm(split(jnp.concatenate([zz, run[N:]], 0)), gs, True)
        for j in range(4):
            at = pl.ds(pl.multiple_of(lax.rem(x + j, 4) * B, B), B)
            cov[2 - k, :, at] = out[:B, j * B : (j + 1) * B]
            mean[pl.ds(8 * (2 - k), 8), at] = out[B : B + 8, j * B : (j + 1) * B]


def T(z, y, c):
    return (z % 4) * 8 + (y % 4) * 2 + c % 2


def tm_move(v, dz=0, dy=0, dc=0):
    perm = [(T(z + dz, y + dy, c + dc), T(z, y, c)) for z in range(4) for y in range(4) for c in range(2)]
    return lax.ppermute(v, "tm", perm)


def x_move(v, d):
    return lax.ppermute(v, "blk", [((i + d) % 4, i) for i in range(4)])


def core_down(v):
    return lax.ppermute(v, "tm", [(i, i + 1) for i in range(0, 32, 2)])


def gather4(u, name):
    v = jnp.concatenate([u[0:B], u[2 * B : 3 * B], u[N:A]], 0)
    out = []
    for d in (1, 2, 3):
        got = tm_move(v, **{name: d})
        right = x_move(got[:B], 1)
        left = x_move(got[:B], -1)
        right = jnp.concatenate([right[:, 3 * B :], right[:, : 3 * B]], 1)
        left = jnp.concatenate([left[:, B:], left[:, :B]], 1)
        out.append(jnp.concatenate([got[:B], right, got[B : 2 * B], left, got[2 * B :]], 0))
    return out


def local(filt_mean, filt_cov, pred_prec, transition):
    x = lax.axis_index("blk")
    t = lax.axis_index("tm")
    z, y, core = t // 8, (t // 2) % 4, t % 2
    roll = lambda v: lax.dynamic_slice_in_dim(jnp.concatenate([v, v], -1), x * B, N, v.ndim - 1)
    cov, prec = roll(filt_cov), roll(pred_prec)
    trans = roll(transition)
    trans = lax.dynamic_slice_in_dim(jnp.concatenate([trans, trans], 0), x * B, N, 0)
    means = jnp.pad(roll(filt_mean)[:, None, :], ((0, 0), (0, 7), (0, 0)))
    core_s = jnp.stack([core, y])

    got = []
    for k in (2, 1, 0):
        c, p = cov[k], prec[k]
        fr = x_move(jnp.concatenate([c[:, : 3 * B], p[:, : 2 * B]], 1), 1)
        fl = x_move(jnp.concatenate([c[:, :B], c[:, 3 * B :], p[:, :B], p[:, 2 * B :]], 1), -1)
        c22 = x_move(fr[:, :B], 1)
        p22 = x_move(fl[:, 2 * B : 3 * B], -1)
        got.append((k, c, p, fr, fl, c22, p22))
    run = ()
    gains, rests = [], []
    for k, c, p, fr, fl, c22, p22 in got:
        flag = jnp.stack([((t == 31) & (k == 2)).astype(jnp.int32)] * 2)
        run = call(
            lambda *a, first=not run: step_kernel(first, *a),
            (sds(N, N), sds(A, N)),
            (flag, c, p, fr, fl, c22, p22, trans, means[k]) + tuple(run),
            [SM] + [VM] * (8 + len(run)),
            (pltpu.VMEM((A, N), F32), pltpu.VMEM((N, N), F32)),
            flops=5 * 3 * 2 * N**3,
            name="step",
        )
        gains.append(run[0])
        rests.append(jnp.concatenate([run[1][:B], run[1][N:A]], 0))
    g, r = run
    g_o, r_o = tm_move(g, dc=1), tm_move(r, dc=1)
    u = call(pair_kernel, sds(A, N), (core_s, g, r, g_o, r_o), [SM] + [VM] * 4, flops=2 * 3 * 2 * N**3, name="pair")

    us = [u] + gather4(u, "dy")
    gs = [core_down(v[:N]) for v in us]
    total, suffix = call(
        plane_kernel,
        (sds(A, N), sds(A, N)),
        (core_s, *us, *gs),
        [SM] + [VM] * 8,
        (pltpu.VMEM((4, A, N), F32), pltpu.VMEM((4, N, N), F32)),
        flops=6 * 3 * 2 * N**3,
        name="plane",
    )
    other = tm_move(suffix, dc=1)
    dg = jnp.where(core == 0, suffix[:N], other[:N])
    dr = jnp.where(core == 0, other, suffix)
    folded = call(
        fold_kernel,
        (sds(N, N),) * 3 + (sds(B + 8, N),) * 3,
        (core_s, *gains, *rests, dg, dr, g_o, r_o),
        [SM] + [VM] * 10,
        (pltpu.VMEM((N, N), F32), pltpu.VMEM((A, N), F32)),
        flops=8 * 3 * 2 * N**3,
        name="fold",
    )
    mine = gather4(total, "dz")
    theirs = [tm_move(v, dc=1) for v in mine]
    zg = [jnp.where(core == 0, a[:N], b[:N]) for a, b in zip(mine[:2], theirs[:2])]
    zr = [jnp.where(core == 0, b, a) for a, b in zip(mine, theirs)]
    smooth_cov, mean = call(
        final_kernel,
        (sds(3, B, N), sds(24, N)),
        (jnp.stack([z, x]), *zg, *zr, *folded),
        [SM] + [VM] * 11,
        flops=6 * 3 * 2 * N**3,
        name="final",
    )
    return mean[::8], smooth_cov


def solution(mesh):
    return jax.shard_map(
        local,
        mesh=mesh,
        in_specs=(P("tm", None), P("tm", "blk", None), P("tm", "blk", None), P()),
        out_specs=(P("tm", None), P("tm", "blk", None)),
        check_vma=False,
    )
```

```python
import functools

import jax
import jax.numpy as jnp
from jax import lax
from jax.experimental import pallas as pl
from jax.experimental.pallas import tpu as pltpu
from jax.sharding import PartitionSpec as P

N = 512
B = 128
H = 256
A = N + 8
F32 = jnp.float32
VM = pl.BlockSpec(memory_space=pltpu.VMEM)
ANY = pl.BlockSpec(memory_space=pl.ANY)
CUT = 216
REST = 208


def split(v):
    hi = v.astype(jnp.bfloat16)
    return hi, (v - hi.astype(F32)).astype(jnp.bfloat16)


def dot(a, b, nt):
    return lax.dot_general(a, b, (((1,), (1 if nt else 0,)), ((), ())), preferred_element_type=F32)


def mm(a, b, nt=False):
    (ah, al), (bh, bl) = a, b
    return dot(ah, bh, nt) + (dot(ah, bl, nt) + dot(al, bh, nt))


def rows(s, lo, hi):
    return s[0][lo:hi], s[1][lo:hi]


def sds(*shape):
    return jax.ShapeDtypeStruct(shape, F32)


def call(body, outs, args, scratch=(), products=0.0, name=None, specs=None):
    return pl.pallas_call(
        body,
        out_shape=outs,
        in_specs=specs or [VM] * len(args),
        out_specs=jax.tree.map(lambda _: VM, outs),
        scratch_shapes=list(scratch),
        compiler_params=pltpu.CompilerParams(vmem_limit_bytes=40 * 2**20),
        cost_estimate=pl.CostEstimate(flops=int(products * 6 * N**3), bytes_accessed=2**20, transcendentals=0),
        name=name,
    )(*args)


def place():
    t = lax.axis_index("tm")
    return t, t // 8, lax.rem(t // 2, 4), lax.rem(t, 2)


def blk(v, j):
    return v[:, j * B : (j + 1) * B]


def prep_kernel(k, cov, prec, c, p, fr, fl, sems):
    x = lax.axis_index("blk")
    todo = []
    for ref, out, order in (
        (cov, c, (0, 1, 2, 3)),
        (prec, p, (0, 1, 2, 3)),
        (cov, fr, (0, 1, 2)),
        (cov, fl, (0, 3)),
    ):
        todo += [(ref, j, out, i) for i, j in enumerate(order)]
    todo += [(prec, 0, fr, 3), (prec, 1, fr, 4), (prec, 0, fl, 2), (prec, 2, fl, 3), (prec, 3, fl, 4)]
    copies = []
    for n, (ref, j, out, i) in enumerate(todo):
        at = pl.ds(pl.multiple_of(lax.rem(x + j, 4) * B, B), B)
        copies.append(pltpu.make_async_copy(ref.at[k, :, at], out.at[:, i * B : (i + 1) * B], sems.at[n]))
    for copy in copies:
        copy.start()
    for copy in copies:
        copy.wait()


def assemble(ref, row, known):
    for j in range(4):
        ref[0:B, j * B : (j + 1) * B] = blk(row, j)
        if j:
            ref[j * B : (j + 1) * B, 0:B] = blk(row, j).T
    for (i, j), block in known.items():
        ref[i * B : (i + 1) * B, j * B : (j + 1) * B] = block
        if i != j:
            ref[j * B : (j + 1) * B, i * B : (i + 1) * B] = block.T


def step_kernel(k, c, p, fr, fl, c22, p22, t, mean, *rest):
    if k == 2:
        go, ro, keep, cf, pf = rest
    else:
        ga, ra, go, ro, keep, cf, pf = rest
    assemble(cf, c, {(1, 1): blk(fr, 0), (1, 2): blk(fr, 1), (1, 3): blk(fr, 2),
                     (3, 3): blk(fl, 0), (3, 2): blk(fl, 1), (2, 2): c22[...]})
    cf[N:A, :] = mean[...]
    assemble(pf, p, {(1, 1): blk(fr, 3), (1, 2): blk(fr, 4), (3, 3): blk(fl, 2),
                     (3, 1): blk(fl, 3), (3, 2): blk(fl, 4), (2, 2): p22[...]})
    n = mm(split(cf[...]), split(t[...]), True)
    if k == 2:
        n = jnp.where(lax.axis_index("tm") == 31, 0.0, n)
    g = mm(split(n[:N]), split(pf[...]))
    gs = split(g)
    if k == 2:
        go[...] = g
        out = cf[...] - mm(split(n), gs, True)
    else:
        go[...] = mm(gs, split(ga[...]))
        r = ra[...]
        z = jnp.concatenate([mm(gs, split(r[:N])), r[N:]], 0) - n
        out = cf[...] + mm(split(z), gs, True)
    ro[...] = out
    keep[0:B] = out[:B]
    keep[B : B + 8] = out[N:]


def write_message(h, g, r, m1, m2):
    m1[...] = g[:CUT]
    n = H - CUT
    m2[0:n] = g[CUT:]
    if h == 0:
        m2[n : n + B] = r[:B]
        odd = r[B:H, B : 2 * B]
    else:
        m2[n : n + B, 0:B] = r[:B, B : 2 * B]
        m2[n : n + B, B:N] = r[B:H, B:N]
        odd = r[:B, 2 * B : 3 * B]
    for q in range(4):
        m2[n + B : n + B + 32, q * B : (q + 1) * B] = odd[32 * q : 32 * (q + 1)]
    m2[n + B + 32 : n + B + 40] = r[H : H + 8]


def read_message(h, m1, m2, g, r):
    n = H - CUT
    if g is not None:
        g[h * H : h * H + CUT] = m1[...]
        g[h * H + CUT : (h + 1) * H] = m2[0:n]
    odd = jnp.concatenate([m2[n + B : n + B + 32, q * B : (q + 1) * B] for q in range(4)], 0)
    if h == 0:
        r[0:B, :] = m2[n : n + B]
        for j in (1, 2, 3):
            r[j * B : (j + 1) * B, 0:B] = m2[n : n + B, j * B : (j + 1) * B].T
        r[B:H, B:H] = odd
        r[N:A, :] = m2[n + B + 32 : n + B + 40]
    else:
        r[3 * B : N, B:N] = m2[n : n + B, B:N]
        r[2 * B : 3 * B, B:H] = m2[n : n + B, 0:B]
        r[2 * B : 3 * B, H : 3 * B] = odd
        r[B:H, H : 3 * B] = m2[n : n + B, 0:B].T
        r[B:H, 3 * B : N] = m2[n : n + B, B:H].T
        r[2 * B : 3 * B, 3 * B : N] = m2[n : n + B, H : 3 * B].T


def read_both(core, own, other, g, r):
    for c in (0, 1):
        @pl.when(core == c)
        def _():
            read_message(c, *own, g, r)
            read_message(1 - c, *other, g, r)


def half(h, g0, r0, g1, r1):
    gs = split(g0)
    gh = rows(gs, h * H, (h + 1) * H)
    g = mm(gh, split(g1))
    z = jnp.concatenate([mm(gh, split(r1[:N])), r1[N:]], 0)
    r = jnp.concatenate([r0[h * H : (h + 1) * H], r0[N:]], 0) + mm(split(z), gs, True)
    return g, r


def apply(gs, s, r):
    z = jnp.concatenate([mm(gs, split(s[:N])), s[N:]], 0)
    return r + mm(split(z), gs, True)


def pair_kernel(g, r, go, ro, m1, m2):
    core = place()[3]

    @pl.when(core == 0)
    def _():
        write_message(0, *half(0, g[...], r[...], go[...], ro[...]), m1, m2)

    @pl.when(core == 1)
    def _():
        write_message(1, *half(1, go[...], ro[...], g[...], r[...]), m1, m2)


def plane_kernel(*refs):
    pieces, (m1, m2, sg, sr, gs, rs) = refs[:16], refs[16:]
    _, _, y, core = place()
    for d in range(4):
        at = lax.rem(y + d, 4)
        read_both(core, pieces[4 * d : 4 * d + 2], pieces[4 * d + 2 : 4 * d + 4], gs.at[at], rs.at[at])
    g, r = gs[3], rs[3]
    eye = lax.broadcasted_iota(jnp.int32, (N, N), 0) == lax.broadcasted_iota(jnp.int32, (N, N), 1)
    sg[...] = jnp.where(y == 3, eye.astype(F32), g)
    sr[...] = jnp.where(y == 3, 0.0, r)
    for i in (2, 1):
        left = split(gs[i])
        g, r = mm(left, split(g)), apply(left, r, rs[i])

        @pl.when(y < i)
        def _():
            sg[...] = g
            sr[...] = r

    for c in (0, 1):
        @pl.when(core == c)
        def _():
            write_message(c, *half(c, gs[0], rs[0], g, r), m1, m2)


def fold_kernel(ga, gb, gc, ra, rb, rc, dg, dr, ge, re, oa, ob, oc, sa, sb, sc, tg, tr):
    core = place()[3]

    @pl.when(core == 0)
    def _():
        g = split(ge[...])
        tg[...] = mm(g, split(dg[...]))
        tr[...] = apply(g, dr[...], re[...])

    @pl.when(core == 1)
    def _():
        tg[...] = dg[...]
        tr[...] = dr[...]

    ds, rs = split(tg[...]), split(tr[0:N])
    for g, r, o, s in ((ga, ra, oa, sa), (gb, rb, ob, sb), (gc, rc, oc, sc)):
        gs = split(g[...])
        o[...] = mm(gs, ds)
        z = jnp.concatenate([mm(rows(gs, 0, B), rs), tr[N:A]], 0)
        s[...] = r[...] + mm(split(z), gs, True)


def final_kernel(*refs):
    pieces, rest = refs[:12], refs[12:]
    (ga, gb, gc, ra, rb, rc, cov, mean, gs, rs) = rest
    _, z, _, core = place()
    x = lax.axis_index("blk")
    for d in range(3):
        read_both(core, pieces[4 * d : 4 * d + 2], pieces[4 * d + 2 : 4 * d + 4], gs.at[d] if d < 2 else None, rs.at[d])
    run = jnp.where(z > 0, 0.0, rs[2])
    for d in (2, 1):
        run = apply(split(gs[d - 1]), run, jnp.where(z + d > 3, 0.0, rs[d - 1]))
    s = split(run[:N])
    for k, g, r in ((2, ga, ra), (1, gb, rb), (0, gc, rc)):
        gk = split(g[...])
        zz = jnp.concatenate([mm(rows(gk, 0, B), s), run[N:]], 0)
        out = r[...] + mm(split(zz), gk, True)
        for j in range(4):
            at = pl.ds(pl.multiple_of(lax.rem(x + j, 4) * B, B), B)
            cov[k, :, at] = out[:B, j * B : (j + 1) * B]
            mean[8 * k : 8 * k + 8, at] = out[B : B + 8, j * B : (j + 1) * B]


def T(z, y, c):
    return (z % 4) * 8 + (y % 4) * 2 + c % 2


def tm_move(v, dz=0, dy=0, dc=0):
    perm = [(T(z + dz, y + dy, c + dc), T(z, y, c)) for z in range(4) for y in range(4) for c in range(2)]
    return lax.ppermute(v, "tm", perm)


def x_move(v, d):
    return lax.ppermute(v, "blk", [((i + d) % 4, i) for i in range(4)])


def swap(v):
    return tm_move(v, dc=1)


def after(first, *then):
    out = lax.optimization_barrier((first, then))
    return out[0], *out[1]


def gather(m1, m2, axis, work=None):
    up, down = {axis: 1}, {axis: -1}
    up1, down2 = tm_move(m1, **up), tm_move(m2, **down)
    up2, down1 = tm_move(m2, **up), tm_move(m1, **down)
    done = work() if work else None
    if work:
        done, up1, down2 = after(done, up1, down2)
    far1, far2 = tm_move(up1, **up), tm_move(down2, **down)
    out = []
    for pair in ((up1, up2), (far1, far2), (down1, down2)):
        out += [*pair, *map(swap, pair)]
    return out, done


def local(filt_mean, filt_cov, pred_prec, transition):
    x = lax.axis_index("blk")
    roll = lambda v, axis: lax.dynamic_slice_in_dim(jnp.concatenate([v, v], axis), x * B, N, axis)
    ready = []
    for k in (2, 1, 0):
        ready.append(call(
            functools.partial(prep_kernel, k),
            (sds(B, N), sds(B, N), sds(B, 5 * B), sds(B, 5 * B)),
            (filt_cov, pred_prec),
            (pltpu.SemaphoreType.DMA((18,)),),
            name="prep",
            specs=[ANY, ANY],
        ))
    trans = roll(roll(transition, 1), 0)
    means = jnp.pad(roll(filt_mean, 1)[:, None, :], ((0, 0), (0, 7), (0, 0)))

    got, last = [], None
    for k, (c, p, fr, fl) in zip((2, 1, 0), ready):
        if last is not None:
            last, fr, fl = after(last, fr, fl)
            got[-1][2:4] = last
        fr, fl = x_move(fr, 1), x_move(fl, -1)
        last = (fr, fl)
        got.append([c, p, fr, fl])
    for item in got:
        fr, fl = item[2:4]
        item += [x_move(blk(fr, 0), 1), x_move(blk(fl, 2), -1)]

    run, gains, rests = (), [], []
    for k, item in zip((2, 1, 0), got):
        *run, keep = call(
            functools.partial(step_kernel, k),
            (sds(N, N), sds(A, N), sds(B + 8, N)),
            (*item, trans, means[k], *run),
            (pltpu.VMEM((A, N), F32), pltpu.VMEM((N, N), F32)),
            products=3 if k == 2 else 5,
            name="step",
        )
        gains.append(run[0])
        rests.append(keep)
    g, r = run
    g_o, r_o = swap(g), swap(r)
    message = (sds(CUT, N), sds(REST, N))
    m = call(pair_kernel, message, (g, r, g_o, r_o), products=1.5, name="pair")

    pieces, _ = gather(*m, "dy")
    *m, sg, sr = call(
        plane_kernel,
        message + (sds(N, N), sds(A, N)),
        (*m, *map(swap, m), *pieces),
        (pltpu.VMEM((4, N, N), F32), pltpu.VMEM((4, A, N), F32)),
        products=7.5,
        name="plane",
    )

    def fold():
        return call(
            fold_kernel,
            (sds(N, N),) * 3 + (sds(B + 8, N),) * 3,
            (*gains, *rests, sg, sr, g_o, r_o),
            (pltpu.VMEM((N, N), F32), pltpu.VMEM((A, N), F32)),
            products=7.5,
            name="fold",
        )

    pieces, folded = gather(*m, "dz", fold)
    smooth_cov, mean = call(
        final_kernel,
        (sds(3, B, N), sds(24, N)),
        (*pieces, *folded),
        (pltpu.VMEM((2, N, N), F32), pltpu.VMEM((3, A, N), F32)),
        products=5.5,
        name="final",
    )
    return mean[::8], smooth_cov


def solution(mesh):
    return jax.shard_map(
        local,
        mesh=mesh,
        in_specs=(P("tm", None), P("tm", "blk", None), P("tm", "blk", None), P()),
        out_specs=(P("tm", None), P("tm", "blk", None)),
        check_vma=False,
    )
```

```python
import functools

import jax
import jax.numpy as jnp
from jax import lax
from jax.experimental import pallas as pl
from jax.experimental.pallas import tpu as pltpu
from jax.sharding import PartitionSpec as P

N = 512
B = 128
H = 256
A = N + 8
F32 = jnp.float32
VM = pl.BlockSpec(memory_space=pltpu.VMEM)
ANY = pl.BlockSpec(memory_space=pl.ANY)
CUT = 216
REST = 208
RM = 168


def split(v):
    hi = v.astype(jnp.bfloat16)
    return hi, (v - hi.astype(F32)).astype(jnp.bfloat16)


def dot(a, b, nt):
    return lax.dot_general(a, b, (((1,), (1 if nt else 0,)), ((), ())), preferred_element_type=F32)


def mm(a, b, nt=False):
    (ah, al), (bh, bl) = a, b
    return dot(ah, bh, nt) + (dot(ah, bl, nt) + dot(al, bh, nt))


def rows(s, lo, hi):
    return s[0][lo:hi], s[1][lo:hi]


def sds(*shape):
    return jax.ShapeDtypeStruct(shape, F32)


def call(body, outs, args, scratch=(), products=0.0, name=None, specs=None, limit=40):
    return pl.pallas_call(
        body,
        out_shape=outs,
        in_specs=specs or [VM] * len(args),
        out_specs=jax.tree.map(lambda _: VM, outs),
        scratch_shapes=list(scratch),
        compiler_params=pltpu.CompilerParams(vmem_limit_bytes=limit * 2**20),
        cost_estimate=pl.CostEstimate(flops=int(products * 6 * N**3) + 1000, bytes_accessed=1000, transcendentals=0),
        name=name,
    )(*args)


def place():
    t = lax.axis_index("tm")
    return t, t // 8, lax.rem(t // 2, 4), lax.rem(t, 2)


def blk(v, j):
    return v[:, j * B : (j + 1) * B]


def at(j):
    return pl.ds(pl.multiple_of(lax.rem(lax.axis_index("blk") + j, 4) * B, B), B)


def prep_kernel(cov, prec, x2, *rest):
    sides, (c, p, sems) = rest[:6], rest[6:]
    copies = []
    for k in (2, 1, 0):
        for src, dst in ((cov, c), (prec, p)):
            copies.append(pltpu.make_async_copy(src.at[k], dst.at[k], sems.at[len(copies)]))
            copies[-1].start()
    for n, k in enumerate((2, 1, 0)):
        copies[2 * n].wait()
        copies[2 * n + 1].wait()
        for out, parts in (
            (x2.at[k], ((c, 0), (p, 0))),
            (sides[2 * k], ((c, 0), (c, 1), (c, 2), (p, 0), (p, 1))),
            (sides[2 * k + 1], ((c, 0), (c, 3), (p, 0), (p, 2), (p, 3))),
        ):
            for i, (v, j) in enumerate(parts):
                out[:, i * B : (i + 1) * B] = v[k, :, at(j)]


def assemble(ref, k, own, known):
    ref[at(0), :] = own[k]
    for j in (1, 2, 3):
        ref[at(j), at(0)] = own[k, :, at(j)].T
    for (i, j), block in known.items():
        ref[at(i), at(j)] = block
        if i != j:
            ref[at(j), at(i)] = block.T


def open_step(k, c, p, fr, fl, x2, t, mean, cf, pf):
    x2 = x2.at[k]
    assemble(cf, k, c, {(1, 1): blk(fr, 0), (1, 2): blk(fr, 1), (1, 3): blk(fr, 2),
                        (3, 3): blk(fl, 0), (3, 2): blk(fl, 1), (2, 2): blk(x2, 0)})
    cf[N:A, :] = mean[...]
    assemble(pf, k, p, {(1, 1): blk(fr, 3), (1, 2): blk(fr, 4), (3, 3): blk(fl, 2),
                        (3, 1): blk(fl, 3), (3, 2): blk(fl, 4), (2, 2): blk(x2, 1)})
    n = mm(split(cf[...]), split(t[...]), True)
    if k == 2:
        n = jnp.where(lax.axis_index("tm") == 31, 0.0, n)
    return n, mm(split(n[:N]), split(pf[...]))


def close_step(c, n, gs, ra, ro, keep):
    r = ra[...]
    z = jnp.concatenate([mm(gs, split(r[:N])), r[N:]], 0) - n
    ro[...] = c + mm(split(z), gs, True)
    keep[0:B] = ro[at(0), :]
    keep[B : B + 8] = ro[N:A]


def first_kernel(*refs):
    go, ro, keep, cf, pf = refs[7:]
    n, g = open_step(2, *refs[:7], cf, pf)
    go[...] = g
    ro[...] = cf[...] - mm(split(n), split(g), True)
    keep[0:B] = ro[at(0), :]
    keep[B : B + 8] = ro[N:A]


def second_kernel(*refs):
    ga, ra, go, ro, keep, cf, pf = refs[7:]
    n, g = open_step(1, *refs[:7], cf, pf)
    gs = split(g)
    go[...] = mm(gs, split(ga[...]))
    close_step(cf[...], n, gs, ra, ro, keep)


def third_kernel(*refs):
    ga, go, no, g0, cf, pf = refs[7:]
    n, g = open_step(0, *refs[:7], cf, pf)
    no[...] = n
    g0[...] = g
    go[...] = mm(split(g), split(ga[...]))


def close_kernel(c, n, g, ra, ro, keep):
    close_step(c[...], n[...], split(g[...]), ra, ro, keep)


def write_rest(h, r, m):
    if h == 0:
        m[0:B] = r[:B]
        odd = r[B:H, B : 2 * B]
    else:
        m[0:B, 0:B] = r[:B, B : 2 * B]
        m[0:B, B:N] = r[B:H, B:N]
        odd = r[:B, 2 * B : 3 * B]
    for q in range(4):
        m[B : B + 32, q * B : (q + 1) * B] = odd[32 * q : 32 * (q + 1)]
    m[B + 32 : RM] = r[H : H + 8]


def read_rest(h, m, r):
    odd = jnp.concatenate([m[B : B + 32, q * B : (q + 1) * B] for q in range(4)], 0)
    if h == 0:
        r[0:B, :] = m[0:B]
        for j in (1, 2, 3):
            r[j * B : (j + 1) * B, 0:B] = m[0:B, j * B : (j + 1) * B].T
        r[B:H, B:H] = odd
        r[N:A, :] = m[B + 32 : RM]
    else:
        r[3 * B : N, B:N] = m[0:B, B:N]
        r[2 * B : 3 * B, B:H] = m[0:B, 0:B]
        r[2 * B : 3 * B, H : 3 * B] = odd
        r[B:H, H : 3 * B] = m[0:B, 0:B].T
        r[B:H, 3 * B : N] = m[0:B, B:H].T
        r[2 * B : 3 * B, 3 * B : N] = m[0:B, H : 3 * B].T


def write_map(h, g, r, m1, m2):
    m1[...] = g[:CUT]
    m2[0 : H - CUT] = g[CUT:]
    write_rest(h, r, m2.at[H - CUT :])


def read_map(h, m1, m2, g, r):
    g[h * H : h * H + CUT] = m1[...]
    g[h * H + CUT : (h + 1) * H] = m2[0 : H - CUT]
    read_rest(h, m2.at[H - CUT :], r)


def both(core, own, other, read):
    for c in (0, 1):
        @pl.when(core == c)
        def _():
            read(c, *own)
            read(1 - c, *other)


def read_maps(core, own, other, g, r):
    both(core, own, other, lambda h, m1, m2: read_map(h, m1, m2, g, r))


def apply(gs, s, r):
    left, right = gs if isinstance(gs[0], tuple) else (gs, gs)
    z = jnp.concatenate([mm(left, split(s[:N])), s[N:]], 0)
    return r + mm(split(z), right, True)


def rows_of(ref, h):
    return jnp.concatenate([ref[h * H : (h + 1) * H], ref[N:A]], 0)


def pair_kernel(g, r, go, ro, m1, m2):
    core = place()[3]

    def half(h, g0, r0, g1, r1):
        gs = split(g0[...])
        gh = rows(gs, h * H, (h + 1) * H)
        write_map(h, mm(gh, split(g1[...])), apply((gh, gs), r1[...], rows_of(r0, h)), m1, m2)

    pl.when(core == 0)(lambda: half(0, g, r, go, ro))
    pl.when(core == 1)(lambda: half(1, go, ro, g, r))


def compose(left, right, out):
    gs = split(left[0][...])
    out[0][...] = mm(gs, split(right[0][...]))
    out[1][...] = apply(gs, right[1][...], left[1][...])


def early_kernel(*refs):
    (own, own_s, up, up_s, down, down_s), rest = [refs[2 * i : 2 * i + 2] for i in range(6)], refs[12:]
    pair, e1, e3, e0 = [rest[2 * i : 2 * i + 2] for i in range(4)]
    _, _, y, core = place()
    read_maps(core, own, own_s, *e0)
    read_maps(core, up, up_s, *e1)
    read_maps(core, down, down_s, *e3)
    even = lax.rem(y, 2) == 0
    pl.when(even)(lambda: compose(e0, e1, pair))
    pl.when(jnp.logical_not(even))(lambda: compose(e3, e0, pair))


def late_kernel(*refs):
    far, far_s, pair, e1, e3, late = [refs[2 * i : 2 * i + 2] for i in range(6)]
    g, gm, r, rm = refs[12:16]
    e2 = refs[16:18]
    _, _, y, core = place()
    read_maps(core, far, far_s, *e2)
    even = lax.rem(y, 2) == 0
    pl.when(even)(lambda: compose(e2, e3, late))
    pl.when(jnp.logical_not(even))(lambda: compose(e1, e2, late))

    def total(left, right):
        gs = split(left[0][...])
        g[...] = mm(gs, split(right[0][...]))
        for c in (0, 1):
            @pl.when(core == c)
            def _():
                gh = rows(gs, c * H, (c + 1) * H)
                r[...] = apply((gh, gs), right[1][...], rows_of(left[1], c))

    pl.when(y < 2)(lambda: total(pair, late))
    pl.when(y >= 2)(lambda: total(late, pair))
    for c in (0, 1):
        @pl.when(core == c)
        def _():
            gm[...] = g[c * H : (c + 1) * H]
            write_rest(c, r[...], rm)


def after_kernel(lg, lr, eg, er, cg, cr, tg, tr, sg, sr):
    _, _, y, core = place()

    def keep(g, r):
        sg[...] = g
        sr[...] = r

    @pl.when(y == 0)
    def _():
        compose((eg, er), (lg, lr), (sg, sr))

    pl.when(y == 1)(lambda: keep(lg[...], lr[...]))
    pl.when(y == 2)(lambda: keep(eg[...], er[...]))

    @pl.when(y == 3)
    def _():
        eye = lax.broadcasted_iota(jnp.int32, (N, N), 0) == lax.broadcasted_iota(jnp.int32, (N, N), 1)
        keep(eye.astype(F32), jnp.zeros((A, N), F32))

    pl.when(core == 0)(lambda: compose((cg, cr), (sg, sr), (tg, tr)))

    @pl.when(core == 1)
    def _():
        tg[...] = sg[...]
        tr[...] = sr[...]


def fold_kernel(ga, gb, gc, ra, rb, rc, tg, tr, oa, ob, oc, sa, sb, sc):
    ds, rs = split(tg[...]), split(tr[0:N])
    for g, r, o, s in ((ga, ra, oa, sa), (gb, rb, ob, sb), (gc, rc, oc, sc)):
        gs = split(g[...])
        o[...] = mm(gs, ds)
        z = jnp.concatenate([mm(split(g[at(0), :]), rs), tr[N:A]], 0)
        s[...] = r[...] + mm(split(z), gs, True)


def next_kernel(g, r, m, m_s, w, rs):
    _, z, _, core = place()
    both(core, (m,), (m_s,), lambda h, v: read_rest(h, v, rs))
    nxt = jnp.where(z == 3, 0.0, rs[...])
    gs = split(g[...])
    for c in (0, 1):
        @pl.when(core == c)
        def _():
            write_rest(c, apply((rows(gs, c * H, (c + 1) * H), gs), nxt, r[...]), w)


def final_kernel(m, m_s, g, g_s, w, w_s, ga, gb, gc, ra, rb, rc, cov, mean, rs, gs, ws):
    _, z, _, core = place()
    both(core, (m, g), (m_s, g_s), lambda h, v, u: (read_rest(h, v, rs), gs.__setitem__(slice(h * H, (h + 1) * H), u[...])))
    both(core, (w,), (w_s,), lambda h, v: read_rest(h, v, ws))
    run = apply(split(gs[...]), jnp.where(z > 1, 0.0, ws[...]), rs[...])
    run = jnp.where(z == 3, 0.0, run)
    s = split(run[:N])
    for k, g, r in ((2, ga, ra), (1, gb, rb), (0, gc, rc)):
        zz = jnp.concatenate([mm(split(g[at(0), :]), s), run[N:]], 0)
        out = r[...] + mm(split(zz), split(g[...]), True)
        cov[k] = out[:B]
        mean[k : k + 1] = out[B : B + 1]


def T(z, y, c):
    return (z % 4) * 8 + (y % 4) * 2 + c % 2


def tm_move(v, dz=0, dy=0, dc=0):
    perm = [(T(z + dz, y + dy, c + dc), T(z, y, c)) for z in range(4) for y in range(4) for c in range(2)]
    return lax.ppermute(v, "tm", perm)


def z_down(v, d, count):
    perm = [(T(z + d, y, c), T(z, y, c)) for z in range(count) for y in range(4) for c in range(2)]
    return lax.ppermute(v, "tm", perm)


def x_move(v, d):
    return lax.ppermute(v, "blk", [((i + d) % 4, i) for i in range(4)])


def swap(v):
    return tm_move(v, dc=1)


def after(first, *then):
    out = lax.optimization_barrier((first, then))
    return out[0], *out[1]


def local(filt_mean, filt_cov, pred_prec, transition):
    means = jnp.pad(filt_mean[:, None, :], ((0, 0), (0, 7), (0, 0)))
    full = (sds(N, N), sds(A, N))
    scratch = (pltpu.VMEM((N, N), F32), pltpu.VMEM((A, N), F32))
    keep = (sds(B + 8, N),)

    opposite, *sides = call(
        prep_kernel,
        (sds(3, B, 2 * B),) + (sds(B, 5 * B),) * 6,
        (filt_cov, pred_prec),
        (pltpu.VMEM((3, B, N), F32), pltpu.VMEM((3, B, N), F32), pltpu.SemaphoreType.DMA((6,))),
        name="prep",
        specs=[ANY, ANY],
        limit=60,
    )
    opposite = x_move(opposite, 2)
    got = {k: (opposite, x_move(sides[2 * k], 1), x_move(sides[2 * k + 1], -1)) for k in (2, 1, 0)}
    args = {k: (filt_cov, pred_prec, got[k][1], got[k][2], got[k][0], transition, means[k]) for k in got}
    back = (scratch[1], scratch[0])
    *run, keep2 = call(first_kernel, full + keep, args[2], back, products=3, name="first")
    g2 = run[0]
    *run, keep1 = call(second_kernel, full + keep, (*args[1], *run), back, products=5, name="second")
    g1 = run[0]
    g, n, g0, c = call(third_kernel, (full[0], full[1], full[0], full[1]), (*args[0], run[0]), scratch[:1], products=3, name="third")
    g_o = swap(g)
    r, keep0 = call(close_kernel, full[1:] + keep, (c, n, g0, run[1]), products=2, name="close")
    r_o = swap(r)
    gains, rests = (g2, g1, g), (keep2, keep1, keep0)
    m1, m2 = call(pair_kernel, (sds(CUT, N), sds(REST, N)), (g, r, g_o, r_o), products=1.5, name="pair")

    up1, down2 = tm_move(m1, dy=1), tm_move(m2, dy=-1)
    swapped, m1, m2 = after((swap(m1), swap(m2)), m1, m2)
    up2, down1 = tm_move(m2, dy=1), tm_move(m1, dy=-1)
    far1, far2 = tm_move(up1, dy=1), tm_move(down2, dy=-1)
    near = (m1, m2, *swapped, up1, up2, swap(up1), swap(up2), down1, down2, swap(down1), swap(down2))
    early = call(early_kernel, full * 3, near, scratch, name="early")
    lg, lr, hg, gm, hr, rm = call(
        late_kernel,
        full + (sds(N, N), sds(H, N), sds(H + 8, N), sds(RM, N)),
        (far1, far2, swap(far1), swap(far2), *early),
        scratch,
        products=5,
        name="late",
    )

    rm = z_down(rm, 1, 3)
    to_end = call(after_kernel, full, (lg, lr, early[2], early[3], g_o, r_o), scratch, name="after")
    to_end, gm = after(to_end, gm)
    to_end, rm = after(to_end, rm)
    gm = z_down(gm, 1, 2)
    rm_s = swap(rm)
    w = call(next_kernel, sds(RM, N), (hg, hr, rm, rm_s), scratch[1:], name="next")
    w = z_down(w, 2, 2)
    folded = call(fold_kernel, full[:1] * 3 + keep * 3, (*gains, *rests, *to_end), name="fold")
    folded, gm = after(folded, gm)
    folded, w = after(folded, w)
    smooth_cov, mean = call(
        final_kernel,
        (sds(3, B, N), sds(3, N)),
        (rm, rm_s, gm, swap(gm), w, swap(w), *folded),
        (scratch[1], scratch[0], scratch[1]),
        products=3.5,
        name="final",
    )
    return mean, smooth_cov


def solution(mesh):
    return jax.shard_map(
        local,
        mesh=mesh,
        in_specs=(P("tm", None), P("tm", "blk", None), P("tm", "blk", None), P()),
        out_specs=(P("tm", None), P("tm", "blk", None)),
        check_vma=False,
    )
```

```python
import functools

import jax
import jax.numpy as jnp
from jax import lax
from jax.experimental import pallas as pl
from jax.experimental.pallas import tpu as pltpu
from jax.sharding import PartitionSpec as P

N = 512
B = 128
H = 256
A = N + 8
F32 = jnp.float32
VM = pl.BlockSpec(memory_space=pltpu.VMEM)
ANY = pl.BlockSpec(memory_space=pl.ANY)
RM = B + 8
MAP = H + RM
CUT = 200


def split(v):
    hi = v.astype(jnp.bfloat16)
    return hi, (v - hi.astype(F32)).astype(jnp.bfloat16)


def dot(a, b, nt):
    return lax.dot_general(a, b, (((1,), (1 if nt else 0,)), ((), ())), preferred_element_type=F32)


def mm(a, b, nt=False):
    (ah, al), (bh, bl) = a, b
    return dot(ah, bh, nt) + (dot(ah, bl, nt) + dot(al, bh, nt))


def rows(s, lo, hi):
    return s[0][lo:hi], s[1][lo:hi]


def sds(*shape):
    return jax.ShapeDtypeStruct(shape, F32)


def call(body, outs, args, scratch=(), products=0.0, name=None, specs=None, limit=40):
    return pl.pallas_call(
        body,
        out_shape=outs,
        in_specs=specs or [VM] * len(args),
        out_specs=jax.tree.map(lambda _: VM, outs),
        scratch_shapes=list(scratch),
        compiler_params=pltpu.CompilerParams(vmem_limit_bytes=limit * 2**20),
        cost_estimate=pl.CostEstimate(flops=int(products * 6 * N**3) + 1000, bytes_accessed=1000, transcendentals=0),
        name=name,
    )(*args)


def place():
    t = lax.axis_index("tm")
    return t, t // 8, lax.rem(t // 2, 4), lax.rem(t, 2)


def blk(v, j):
    return v[:, j * B : (j + 1) * B]


def at(j):
    return pl.ds(pl.multiple_of(lax.rem(lax.axis_index("blk") + j, 4) * B, B), B)


def places():
    return lax.broadcasted_iota(jnp.int32, (B, B), 0), lax.broadcasted_iota(jnp.int32, (B, B), 1)


def pack(a, b):
    i, j = places()
    return jnp.where(i <= j, a, b), jnp.sum(jnp.where(i == j, b, 0.0), 0, keepdims=True)


def unpack(both, diagonal):
    i, j = places()
    turned = both.T
    return jnp.where(i <= j, both, turned), jnp.where(i > j, both, jnp.where(i < j, turned, diagonal))


def prep_kernel(cov, prec, opposite, *rest):
    sides, (c, p, sems) = rest[:6], rest[6:]
    copies = []
    for k in (2, 1, 0):
        for src, dst in ((cov, c), (prec, p)):
            copies.append(pltpu.make_async_copy(src.at[k], dst.at[k], sems.at[len(copies)]))
            copies[-1].start()
    for n, k in enumerate((2, 1, 0)):
        copies[2 * n].wait()
        copies[2 * n + 1].wait()
        x2, fr, fl = opposite.at[k], sides[2 * k], sides[2 * k + 1]
        packed, diagonal = pack(c[k, :, at(0)], p[k, :, at(0)])
        diagonal = jnp.broadcast_to(diagonal, (8, B))
        for out in (x2, fr, fl):
            out[0:B, 0:B] = packed
            out[B:RM, 0:B] = diagonal
        for out, parts in ((fr, ((c, 1), (c, 2), (p, 1))), (fl, ((c, 3), (p, 2), (p, 3)))):
            out[B:RM, B:N] = jnp.zeros((8, N - B), F32)
            for i, (v, j) in enumerate(parts):
                out[0:B, (i + 1) * B : (i + 2) * B] = v[k, :, at(j)]


def split_kernel(t, hi, lo, v, sem):
    copy = pltpu.make_async_copy(t, v, sem)
    copy.start()
    copy.wait()
    hi[...], lo[...] = split(v[...])


def assemble(ref, k, own, known):
    ref[at(0), :] = own[k]
    for j in (1, 2, 3):
        ref[at(j), at(0)] = own[k, :, at(j)].T
    for (i, j), block in known.items():
        ref[at(i), at(j)] = block
        if i != j:
            ref[at(j), at(i)] = block.T


def open_step(k, c, p, fr, fl, x2, hi, lo, mean, cf, pf):
    x2 = x2.at[k]
    (c1, p1), (c2, p2), (c3, p3) = (unpack(v[0:B, 0:B], v[B : B + 1, 0:B]) for v in (fr, x2, fl))
    fr, fl = ([v[0:B, i * B : (i + 1) * B] for i in (1, 2, 3)] for v in (fr, fl))
    assemble(cf, k, c, {(1, 1): c1, (1, 2): fr[0], (1, 3): fr[1], (3, 3): c3, (3, 2): fl[0], (2, 2): c2})
    cf[N:A, :] = mean[...]
    assemble(pf, k, p, {(1, 1): p1, (1, 2): fr[2], (3, 3): p3, (3, 1): fl[1], (3, 2): fl[2], (2, 2): p2})
    n = mm(split(cf[...]), (hi[...], lo[...]), True)
    if k == 2:
        n = jnp.where(lax.axis_index("tm") == 31, 0.0, n)
    return n, mm(split(n[:N]), split(pf[...]))


def close_step(c, n, gs, ra, ro, keep):
    r = ra[...]
    z = jnp.concatenate([mm(gs, split(r[:N])), r[N:]], 0) - n
    ro[...] = c + mm(split(z), gs, True)
    keep[0:B] = ro[at(0), :]
    keep[B : B + 8] = ro[N:A]


def first_kernel(*refs):
    go, ro, keep, cf, pf = refs[8:]
    n, g = open_step(2, *refs[:8], cf, pf)
    go[...] = g
    ro[...] = cf[...] - mm(split(n), split(g), True)
    keep[0:B] = ro[at(0), :]
    keep[B : B + 8] = ro[N:A]


def second_kernel(*refs):
    ga, ra, go, ro, keep, cf, pf = refs[8:]
    n, g = open_step(1, *refs[:8], cf, pf)
    gs = split(g)
    go[...] = mm(gs, split(ga[...]))
    close_step(cf[...], n, gs, ra, ro, keep)


def third_kernel(*refs):
    ga, go, no, g0, cf, pf = refs[8:]
    n, g = open_step(0, *refs[:8], cf, pf)
    no[...] = n
    g0[...] = g
    go[...] = mm(split(g), split(ga[...]))


def close_kernel(c, n, g, ra, ro, keep):
    close_step(c[...], n[...], split(g[...]), ra, ro, keep)


def write_rest(h, r, m):
    if h == 0:
        packed, diagonal = pack(r[:B, :B], r[B:H, B:H])
        m[0:B, 0:B] = packed
        m[0:B, B:N] = r[:B, B:N]
    else:
        packed, diagonal = pack(r[B:H, 3 * B : N], r[:B, H : 3 * B])
        m[0:B, 0:B] = r[:B, B:H]
        m[0:B, B : 3 * B] = r[B:H, B : 3 * B]
        m[0:B, 3 * B : N] = packed
    row = lax.broadcasted_iota(jnp.int32, (8, B), 0)
    m[B:RM, 0:B] = jnp.where(row == 1, diagonal, r[H : H + 8, 0:B])
    m[B:RM, B:N] = r[H : H + 8, B:N]


def read_rest(h, m, r):
    diagonal = m[B + 1 : B + 2, 0:B]
    if h == 0:
        r[0:B, 0:B], r[B:H, B:H] = unpack(m[0:B, 0:B], diagonal)
        r[0:B, B:N] = m[0:B, B:N]
        for j in (1, 2, 3):
            r[j * B : (j + 1) * B, 0:B] = m[0:B, j * B : (j + 1) * B].T
        r[N:A, :] = jnp.where(lax.broadcasted_iota(jnp.int32, (8, N), 0) == 0, m[B:RM], 0.0)
    else:
        r[3 * B : N, 3 * B : N], r[H : 3 * B, H : 3 * B] = unpack(m[0:B, 3 * B : N], diagonal)
        r[3 * B : N, B : 3 * B] = m[0:B, B : 3 * B]
        r[H : 3 * B, B:H] = m[0:B, 0:B]
        r[B:H, H : 3 * B] = m[0:B, 0:B].T
        r[B:H, 3 * B : N] = m[0:B, B:H].T
        r[H : 3 * B, 3 * B : N] = m[0:B, H : 3 * B].T


def write_map(h, g, r, m):
    m[0:H] = g
    write_rest(h, r, m.at[H:MAP])


def read_map(h, m, g, r):
    g[h * H : (h + 1) * H] = m[0:H]
    read_rest(h, m.at[H:MAP], r)


def both(core, own, other, read):
    for c in (0, 1):
        @pl.when(core == c)
        def _():
            read(c, *own)
            read(1 - c, *other)


def read_maps(core, own, other, g, r):
    both(core, (own,), (other,), lambda h, m: read_map(h, m, g, r))


def apply(gs, s, r):
    left, right = gs if isinstance(gs[0], tuple) else (gs, gs)
    z = jnp.concatenate([mm(left, split(s[:N])), s[N:]], 0)
    return r + mm(split(z), right, True)


def rows_of(ref, h):
    return jnp.concatenate([ref[h * H : (h + 1) * H], ref[N:A]], 0)


def pair_kernel(g, r, go, ro, m):
    core = place()[3]

    def half(h, g0, r0, g1, r1):
        gs = split(g0[...])
        gh = rows(gs, h * H, (h + 1) * H)
        write_map(h, mm(gh, split(g1[...])), apply((gh, gs), r1[...], rows_of(r0, h)), m)

    pl.when(core == 0)(lambda: half(0, g, r, go, ro))
    pl.when(core == 1)(lambda: half(1, go, ro, g, r))


def compose(left, right, out):
    gs = split(left[0][...])
    out[0][...] = mm(gs, split(right[0][...]))
    out[1][...] = apply(gs, right[1][...], left[1][...])


def early_kernel(*refs):
    own, own_s, up, up_s, down, down_s = refs[:6]
    pair, e1, e3, e0 = [refs[2 * i : 2 * i + 2] for i in (3, 4, 5, 6)]
    _, _, y, core = place()
    read_maps(core, own, own_s, *e0)
    read_maps(core, up, up_s, *e1)
    read_maps(core, down, down_s, *e3)
    even = lax.rem(y, 2) == 0
    pl.when(even)(lambda: compose(e0, e1, pair))
    pl.when(jnp.logical_not(even))(lambda: compose(e3, e0, pair))


def late_kernel(*refs):
    far, far_s, pair, e1, e3, late = [refs[2 * i : 2 * i + 2] for i in range(6)]
    g, gm, r, rm = refs[12:16]
    e2, (m, m_s) = refs[16:18], refs[18:]
    _, _, y, core = place()
    for v, (a, b) in ((m, far), (m_s, far_s)):
        v[0:CUT] = a[...]
        v[CUT:MAP] = b[...]
    read_maps(core, m, m_s, *e2)
    even = lax.rem(y, 2) == 0
    pl.when(even)(lambda: compose(e2, e3, late))
    pl.when(jnp.logical_not(even))(lambda: compose(e1, e2, late))

    def total(left, right):
        gs = split(left[0][...])
        g[...] = mm(gs, split(right[0][...]))
        for c in (0, 1):
            @pl.when(core == c)
            def _():
                gh = rows(gs, c * H, (c + 1) * H)
                r[...] = apply((gh, gs), right[1][...], rows_of(left[1], c))

    pl.when(y < 2)(lambda: total(pair, late))
    pl.when(y >= 2)(lambda: total(late, pair))
    for c in (0, 1):
        @pl.when(core == c)
        def _():
            gm[...] = g[c * H : (c + 1) * H]
            write_rest(c, r[...], rm)


def after_kernel(lg, lr, eg, er, cg, cr, tg, tr, sg, sr):
    _, _, y, core = place()

    def keep(g, r):
        sg[...] = g
        sr[...] = r

    @pl.when(y == 0)
    def _():
        compose((eg, er), (lg, lr), (sg, sr))

    pl.when(y == 1)(lambda: keep(lg[...], lr[...]))
    pl.when(y == 2)(lambda: keep(eg[...], er[...]))

    @pl.when(y == 3)
    def _():
        eye = lax.broadcasted_iota(jnp.int32, (N, N), 0) == lax.broadcasted_iota(jnp.int32, (N, N), 1)
        keep(eye.astype(F32), jnp.zeros((A, N), F32))

    pl.when(core == 0)(lambda: compose((cg, cr), (sg, sr), (tg, tr)))

    @pl.when(core == 1)
    def _():
        tg[...] = sg[...]
        tr[...] = sr[...]


def fold_kernel(ga, gb, gc, ra, rb, rc, tg, tr, oa, ob, oc, sa, sb, sc):
    ds, rs = split(tg[...]), split(tr[0:N])
    for g, r, o, s in ((ga, ra, oa, sa), (gb, rb, ob, sb), (gc, rc, oc, sc)):
        gs = split(g[...])
        o[...] = mm(gs, ds)
        z = jnp.concatenate([mm(split(g[at(0), :]), rs), tr[N:A]], 0)
        s[...] = r[...] + mm(split(z), gs, True)


def next_kernel(g, r, m, m_s, w, rs):
    _, z, _, core = place()

    @pl.when(z == 2)
    def _():
        both(core, (m,), (m_s,), lambda h, v: read_rest(h, v, rs))
        gs = split(g[...])
        for c in (0, 1):
            @pl.when(core == c)
            def _():
                write_rest(c, apply((rows(gs, c * H, (c + 1) * H), gs), rs[...], r[...]), w)

    @pl.when(z != 2)
    def _():
        w[...] = jnp.zeros((RM, N), F32)


def final_kernel(m, m_s, g, g_s, w, w_s, ga, gb, gc, ra, rb, rc, cov, mean, rs, gs, ws):
    _, z, _, core = place()

    @pl.when(z != 1)
    def _():
        both(core, (m,), (m_s,), lambda h, v: read_rest(h, v, rs))

    @pl.when(z == 1)
    def _():
        both(core, (w,), (w_s,), lambda h, v: read_rest(h, v, rs))

    @pl.when(z == 0)
    def _():
        both(core, (w,), (w_s,), lambda h, v: read_rest(h, v, ws))
        both(core, (g,), (g_s,), lambda h, v: gs.__setitem__(slice(h * H, (h + 1) * H), v[...]))
        rs[...] = apply(split(gs[...]), ws[...], rs[...])

    run = jnp.where(z == 3, 0.0, rs[...])
    s = split(run[:N])
    for k, g, r in ((2, ga, ra), (1, gb, rb), (0, gc, rc)):
        zz = jnp.concatenate([mm(split(g[at(0), :]), s), run[N:]], 0)
        out = r[...] + mm(split(zz), split(g[...]), True)
        cov[k] = out[:B]
        mean[k : k + 1] = out[B : B + 1]


def T(z, y, c):
    return (z % 4) * 8 + (y % 4) * 2 + c % 2


def tm_move(v, dz=0, dy=0, dc=0):
    perm = [(T(z + dz, y + dy, c + dc), T(z, y, c)) for z in range(4) for y in range(4) for c in range(2)]
    return lax.ppermute(v, "tm", perm)


def z_move(v, *pairs):
    perm = [(T(a, y, c), T(b, y, c)) for a, b in pairs for y in range(4) for c in range(2)]
    return lax.ppermute(v, "tm", perm)


def x_move(v, d):
    return lax.ppermute(v, "blk", [((i + d) % 4, i) for i in range(4)])


def swap(v):
    return tm_move(v, dc=1)


def after(first, *then):
    out = lax.optimization_barrier((first, then))
    return out[0], *out[1]


def local(filt_mean, filt_cov, pred_prec, transition):
    means = jnp.pad(filt_mean[:, None, :], ((0, 0), (0, 7), (0, 0)))
    full = (sds(N, N), sds(A, N))
    scratch = (pltpu.VMEM((N, N), F32), pltpu.VMEM((A, N), F32))
    keep = (sds(B + 8, N),)

    opposite, *sides = call(
        prep_kernel,
        (sds(3, RM, B),) + (sds(RM, N),) * 6,
        (filt_cov, pred_prec),
        (pltpu.VMEM((3, B, N), F32), pltpu.VMEM((3, B, N), F32), pltpu.SemaphoreType.DMA((6,))),
        name="prep",
        specs=[ANY, ANY],
        limit=60,
    )
    opposite = x_move(opposite, 2)
    got = {k: (opposite, x_move(sides[2 * k], 1), x_move(sides[2 * k + 1], -1)) for k in (2, 1, 0)}
    half = jax.ShapeDtypeStruct((N, N), jnp.bfloat16)
    trans = call(
        split_kernel,
        (half, half),
        (transition,),
        (pltpu.VMEM((N, N), F32), pltpu.SemaphoreType.DMA),
        products=3,
        name="split",
        specs=[ANY],
    )
    args = {k: (filt_cov, pred_prec, got[k][1], got[k][2], got[k][0], *trans, means[k]) for k in got}
    back = (scratch[1], scratch[0])
    *run, keep2 = call(first_kernel, full + keep, args[2], back, products=3, name="first")
    g2 = run[0]
    *run, keep1 = call(second_kernel, full + keep, (*args[1], *run), back, products=5, name="second")
    g1 = run[0]
    g, n, g0, c = call(third_kernel, (full[0], full[1], full[0], full[1]), (*args[0], run[0]), scratch[:1], products=3, name="third")
    g_o = swap(g)
    r, keep0 = call(close_kernel, full[1:] + keep, (c, n, g0, run[1]), products=2, name="close")
    r_o = swap(r)
    gains, rests = (g2, g1, g), (keep2, keep1, keep0)
    m = call(pair_kernel, sds(MAP, N), (g, r, g_o, r_o), name="pair")

    up, down = tm_move(m, dy=1), tm_move(m, dy=-1)
    far1, far2 = tm_move(up[:CUT], dy=1), tm_move(down[CUT:], dy=-1)
    near = (m, swap(m), up, swap(up), down, swap(down))
    early = call(early_kernel, full * 3, near, scratch, name="early")
    lg, lr, hg, gm, hr, rm = call(
        late_kernel,
        full + (sds(N, N), sds(H, N), sds(H + 8, N), sds(RM, N)),
        (far1, far2, swap(far1), swap(far2), *early),
        scratch + (pltpu.VMEM((MAP, N), F32), pltpu.VMEM((MAP, N), F32)),
        products=5,
        name="late",
    )

    rm = z_move(rm, (3, 2), (1, 0))
    to_end = call(after_kernel, full, (lg, lr, early[2], early[3], g_o, r_o), scratch, name="after")
    to_end, gm = after(to_end, gm)
    to_end, rm = after(to_end, rm)
    gm = z_move(gm, (1, 0))
    rm_s = swap(rm)
    w = call(next_kernel, sds(RM, N), (hg, hr, rm, rm_s), scratch[1:], name="next")
    w = z_move(w, (2, 0)) + z_move(w, (2, 1))
    folded = call(fold_kernel, full[:1] * 3 + keep * 3, (*gains, *rests, *to_end), name="fold")
    folded, gm = after(folded, gm)
    folded, w = after(folded, w)
    smooth_cov, mean = call(
        final_kernel,
        (sds(3, B, N), sds(3, N)),
        (rm, rm_s, gm, swap(gm), w, swap(w), *folded),
        (scratch[1], scratch[0], scratch[1]),
        products=3.5,
        name="final",
    )
    return mean, smooth_cov


def solution(mesh):
    return jax.shard_map(
        local,
        mesh=mesh,
        in_specs=(P("tm", None), P("tm", "blk", None), P("tm", "blk", None), P()),
        out_specs=(P("tm", None), P("tm", "blk", None)),
        check_vma=False,
    )
```

```python
import functools

import jax
import jax.numpy as jnp
from jax import lax
from jax.experimental import pallas as pl
from jax.experimental.pallas import tpu as pltpu
from jax.sharding import PartitionSpec as P

N = 512
B = 128
H = 256
A = N + 8
F32 = jnp.float32
VM = pl.BlockSpec(memory_space=pltpu.VMEM)
ANY = pl.BlockSpec(memory_space=pl.ANY)
RM = B + 8
CUT = 64


def split(v):
    hi = v.astype(jnp.bfloat16)
    return hi, (v - hi.astype(F32)).astype(jnp.bfloat16)


def dot(a, b, nt):
    return lax.dot_general(a, b, (((1,), (1 if nt else 0,)), ((), ())), preferred_element_type=F32)


def mm(a, b, nt=False):
    (ah, al), (bh, bl) = a, b
    return dot(ah, bh, nt) + (dot(ah, bl, nt) + dot(al, bh, nt))


def rows(s, lo, hi):
    return s[0][lo:hi], s[1][lo:hi]


def sds(*shape):
    return jax.ShapeDtypeStruct(shape, F32)


def call(body, outs, args, scratch=(), products=0.0, name=None, specs=None, limit=24, aliases=None):
    return pl.pallas_call(
        body,
        out_shape=outs,
        in_specs=specs or [VM] * len(args),
        out_specs=jax.tree.map(lambda _: VM, outs),
        scratch_shapes=list(scratch),
        input_output_aliases=aliases or {},
        compiler_params=pltpu.CompilerParams(vmem_limit_bytes=limit * 2**20),
        cost_estimate=pl.CostEstimate(flops=int(products * 6 * N**3) + 1000, bytes_accessed=1000, transcendentals=0),
        name=name,
    )(*args)


def place():
    t = lax.axis_index("tm")
    return t, t // 8, lax.rem(t // 2, 4), lax.rem(t, 2)


def blk(v, j):
    return v[:, j * B : (j + 1) * B]


def at(j):
    return pl.ds(pl.multiple_of(lax.rem(lax.axis_index("blk") + j, 4) * B, B), B)


def places():
    return lax.broadcasted_iota(jnp.int32, (B, B), 0), lax.broadcasted_iota(jnp.int32, (B, B), 1)


def pack(a, b):
    i, j = places()
    return jnp.where(i <= j, a, b), jnp.sum(jnp.where(i == j, b, 0.0), 0, keepdims=True)


def unpack(both, diagonal):
    i, j = places()
    turned = both.T
    return jnp.where(i <= j, both, turned), jnp.where(i > j, both, jnp.where(i < j, turned, diagonal))


def prep_kernel(cov, prec, opposite, *rest):
    sides, (c, p, sems) = rest[:6], rest[6:]
    copies = []
    for k in (2, 1, 0):
        for src, dst in ((cov, c), (prec, p)):
            copies.append(pltpu.make_async_copy(src.at[k], dst.at[k], sems.at[len(copies)]))
            copies[-1].start()
    for n, k in enumerate((2, 1, 0)):
        copies[2 * n].wait()
        copies[2 * n + 1].wait()
        x2, fr, fl = opposite.at[k], sides[2 * k], sides[2 * k + 1]
        packed, diagonal = pack(c[k, :, at(0)], p[k, :, at(0)])
        diagonal = jnp.broadcast_to(diagonal, (8, B))
        for out in (x2, fr, fl):
            out[0:B, 0:B] = packed
            out[B:RM, 0:B] = diagonal
        for out, parts in ((fr, ((c, 1), (c, 2), (p, 1))), (fl, ((c, 3), (p, 2), (p, 3)))):
            out[B:RM, B:N] = jnp.zeros((8, N - B), F32)
            for i, (v, j) in enumerate(parts):
                out[0:B, (i + 1) * B : (i + 2) * B] = v[k, :, at(j)]


def split_kernel(t, hi, lo, v, sem):
    copy = pltpu.make_async_copy(t, v, sem)
    copy.start()
    copy.wait()
    hi[...], lo[...] = split(v[...])


def assemble(ref, k, own, known):
    ref[at(0), :] = own[k]
    for j in (1, 2, 3):
        ref[at(j), at(0)] = own[k, :, at(j)].T
    for (i, j), block in known.items():
        ref[at(i), at(j)] = block
        if i != j:
            ref[at(j), at(i)] = block.T


def open_step(k, c, p, fr, fl, x2, hi, lo, mean, cf, pf):
    x2 = x2.at[k]
    (c1, p1), (c2, p2), (c3, p3) = (unpack(v[0:B, 0:B], v[B : B + 1, 0:B]) for v in (fr, x2, fl))
    fr, fl = ([v[0:B, i * B : (i + 1) * B] for i in (1, 2, 3)] for v in (fr, fl))
    assemble(cf, k, c, {(1, 1): c1, (1, 2): fr[0], (1, 3): fr[1], (3, 3): c3, (3, 2): fl[0], (2, 2): c2})
    cf[N:A, :] = mean[...]
    assemble(pf, k, p, {(1, 1): p1, (1, 2): fr[2], (3, 3): p3, (3, 1): fl[1], (3, 2): fl[2], (2, 2): p2})
    n = mm(split(cf[...]), (hi[...], lo[...]), True)
    if k == 2:
        n = jnp.where(lax.axis_index("tm") == 31, 0.0, n)
    return n, mm(split(n[:N]), split(pf[...]))


def close_step(c, n, gs, ra, ro, keep):
    r = ra[...]
    z = jnp.concatenate([mm(gs, split(r[:N])), r[N:]], 0) - n
    ro[...] = c + mm(split(z), gs, True)
    keep[0:B] = ro[at(0), :]
    keep[B : B + 8] = ro[N:A]


def first_kernel(*refs):
    go, ro, keep, cf, pf = refs[8:]
    n, g = open_step(2, *refs[:8], cf, pf)
    go[...] = g
    ro[...] = cf[...] - mm(split(n), split(g), True)
    keep[0:B] = ro[at(0), :]
    keep[B : B + 8] = ro[N:A]


def second_kernel(*refs):
    ga, ra, go, ro, keep, cf, pf = refs[8:]
    n, g = open_step(1, *refs[:8], cf, pf)
    gs = split(g)
    go[...] = mm(gs, split(ga[...]))
    close_step(cf[...], n, gs, ra, ro, keep)


def third_kernel(*refs):
    ga, go, no, g0, cf, pf = refs[8:]
    n, g = open_step(0, *refs[:8], cf, pf)
    no[...] = n
    g0[...] = g
    go[...] = mm(split(g), split(ga[...]))


def close_kernel(c, n, g, ra, ro, keep, packed):
    close_step(c[...], n[...], split(g[...]), ra, ro, keep)
    for h in (0, 1):
        write_rest(h, rows_of(ro, h), packed.at[h])


def write_rest(h, r, m):
    if h == 0:
        packed, diagonal = pack(r[:B, :B], r[B:H, B:H])
        m[0:B, 0:B] = packed
        m[0:B, B:N] = r[:B, B:N]
    else:
        packed, diagonal = pack(r[B:H, 3 * B : N], r[:B, H : 3 * B])
        m[0:B, 0:B] = r[:B, B:H]
        m[0:B, B : 3 * B] = r[B:H, B : 3 * B]
        m[0:B, 3 * B : N] = packed
    row = lax.broadcasted_iota(jnp.int32, (8, B), 0)
    m[B:RM, 0:B] = jnp.where(row == 1, diagonal, r[H : H + 8, 0:B])
    m[B:RM, B:N] = r[H : H + 8, B:N]


def read_rest(h, m, r):
    diagonal = m[B + 1 : B + 2, 0:B]
    if h == 0:
        r[0:B, 0:B], r[B:H, B:H] = unpack(m[0:B, 0:B], diagonal)
        r[0:B, B:N] = m[0:B, B:N]
        for j in (1, 2, 3):
            r[j * B : (j + 1) * B, 0:B] = m[0:B, j * B : (j + 1) * B].T
        r[N:A, :] = jnp.where(lax.broadcasted_iota(jnp.int32, (8, N), 0) == 0, m[B:RM], 0.0)
    else:
        r[3 * B : N, 3 * B : N], r[H : 3 * B, H : 3 * B] = unpack(m[0:B, 3 * B : N], diagonal)
        r[3 * B : N, B : 3 * B] = m[0:B, B : 3 * B]
        r[H : 3 * B, B:H] = m[0:B, 0:B]
        r[B:H, H : 3 * B] = m[0:B, 0:B].T
        r[B:H, 3 * B : N] = m[0:B, B:H].T
        r[H : 3 * B, 3 * B : N] = m[0:B, H : 3 * B].T


def read_map(h, mg, mr, g, r):
    g[h * H : (h + 1) * H] = mg[...]
    read_rest(h, mr, r)


def both(core, own, other, read):
    for c in (0, 1):
        @pl.when(core == c)
        def _():
            read(c, *own)
            read(1 - c, *other)


def read_maps(core, own, other, g, r):
    both(core, own, other, lambda h, mg, mr: read_map(h, mg, mr, g, r))


def apply(gs, s, r):
    left, right = gs if isinstance(gs[0], tuple) else (gs, gs)
    z = jnp.concatenate([mm(left, split(s[:N])), s[N:]], 0)
    return r + mm(split(z), right, True)


def rows_of(ref, h):
    return jnp.concatenate([ref[h * H : (h + 1) * H], ref[N:A]], 0)


def pair_gain_kernel(g, go, mg):
    core = place()[3]

    def half(h, g0, g1):
        mg[...] = mm(split(g0[h * H : (h + 1) * H]), split(g1[...]))

    pl.when(core == 0)(lambda: half(0, g, go))
    pl.when(core == 1)(lambda: half(1, go, g))


def pair_rest_kernel(g, r, go, packed, mr, ro):
    core = place()[3]
    for h in (0, 1):
        read_rest(h, packed.at[h], ro)

    def half(h, g0, r0, r1):
        gs = split(g0[...])
        write_rest(h, apply((rows(gs, h * H, (h + 1) * H), gs), r1[...], rows_of(r0, h)), mr)

    pl.when(core == 0)(lambda: half(0, g, r, ro))
    pl.when(core == 1)(lambda: half(1, go, ro, r))


def compose(left, right, out):
    gs = split(left[0][...])
    out[0][...] = mm(gs, split(right[0][...]))
    out[1][...] = apply(gs, right[1][...], left[1][...])


def early_kernel(*refs):
    own, own_s, up, up_s, down, down_s, maps = [refs[2 * i : 2 * i + 2] for i in range(7)]
    _, _, y, core = place()
    slot = lambda i: (maps[0].at[i], maps[1].at[i])
    read_maps(core, own, own_s, *slot(3))
    read_maps(core, up, up_s, *slot(1))
    read_maps(core, down, down_s, *slot(2))
    even = lax.rem(y, 2) == 0
    compose(slot(jnp.where(even, 3, 2)), slot(jnp.where(even, 1, 3)), slot(0))


def order():
    y = place()[2]
    pick = lambda a, b, c, d: jnp.where(y == 0, a, jnp.where(y == 1, b, jnp.where(y == 2, c, d)))
    return pick(0, 0, 3, 1), pick(3, 1, 2, 3), pick(2, 3, 0, 0)


def late_kernel(*refs):
    far, far_s, (old_g, old_r, g, r, inner, own, rm) = refs[0:2], refs[2:4], refs[4:]
    core = place()[3]

    def read(h, upper, lower):
        g[3, h * H : h * H + CUT] = upper[0:CUT]
        g[3, h * H + CUT : (h + 1) * H] = lower[...]
        read_rest(h, upper.at[CUT : CUT + RM], r.at[3])

    both(core, far, far_s, read)
    first, second, third = order()
    inner[...] = apply(split(g[second]), r[third], r[second])
    gs = split(g[first])
    half = pl.ds(pl.multiple_of(core * H, H), H)
    add = jnp.concatenate([r[first, half, :], r[first, N:A, :]], 0)
    own[...] = apply((split(g[first, half, :]), gs), inner[...], add)
    for c in (0, 1):
        @pl.when(core == c)
        def _():
            write_rest(c, own[...], rm)


def gain_kernel(g, inner, hi, lo, gm):
    core = place()[3]
    first, second, third = order()
    inner[...] = mm(split(g[second]), split(g[third]))
    total = mm(split(g[first]), split(inner[...]))
    hi[...], lo[...] = split(total)
    for c in (0, 1):
        @pl.when(core == c)
        def _():
            gm[...] = total[c * H : (c + 1) * H]


def after_kernel(lg, lr, g, r, cg, cr, tg, tr, sg, sr):
    _, _, y, core = place()
    eg, er = g.at[1], r.at[1]

    def keep(g, r):
        sg[...] = g
        sr[...] = r

    @pl.when(y == 0)
    def _():
        compose((eg, er), (lg, lr), (sg, sr))

    pl.when(y == 1)(lambda: keep(lg[...], lr[...]))
    pl.when(y == 2)(lambda: keep(eg[...], er[...]))

    @pl.when(y == 3)
    def _():
        eye = lax.broadcasted_iota(jnp.int32, (N, N), 0) == lax.broadcasted_iota(jnp.int32, (N, N), 1)
        keep(eye.astype(F32), jnp.zeros((A, N), F32))

    pl.when(core == 0)(lambda: compose((cg, cr), (sg, sr), (tg, tr)))

    @pl.when(core == 1)
    def _():
        tg[...] = sg[...]
        tr[...] = sr[...]


def fold_kernel(ga, gb, gc, ra, rb, rc, tg, tr, *out):
    ds, rs = split(tg[...]), split(tr[0:N])
    for i, (g, r) in enumerate(((ga, ra), (gb, rb), (gc, rc))):
        hi, lo, s = out[3 * i : 3 * i + 3]
        gs = split(g[...])
        hi[...], lo[...] = split(mm(gs, ds))
        z = jnp.concatenate([mm(split(g[at(0), :]), rs), tr[N:A]], 0)
        s[...] = r[...] + mm(split(z), gs, True)


def next_kernel(hi, lo, r, m, m_s, w, rs):
    _, z, _, core = place()

    @pl.when(z == 2)
    def _():
        both(core, (m,), (m_s,), lambda h, v: read_rest(h, v, rs))
        gs = hi[...], lo[...]
        for c in (0, 1):
            @pl.when(core == c)
            def _():
                write_rest(c, apply((rows(gs, c * H, (c + 1) * H), gs), rs[...], r[...]), w)

    @pl.when(z != 2)
    def _():
        w[...] = jnp.zeros((RM, N), F32)


def final_kernel(m, m_s, g, g_s, w, w_s, *refs):
    steps, (cov, mean, rs, gs, ws) = [refs[3 * i : 3 * i + 3] for i in range(3)], refs[9:]
    _, z, _, core = place()

    @pl.when(z != 1)
    def _():
        both(core, (m,), (m_s,), lambda h, v: read_rest(h, v, rs))

    @pl.when(z == 1)
    def _():
        both(core, (w,), (w_s,), lambda h, v: read_rest(h, v, rs))

    @pl.when(z == 0)
    def _():
        both(core, (w,), (w_s,), lambda h, v: read_rest(h, v, ws))
        both(core, (g,), (g_s,), lambda h, v: gs.__setitem__(slice(h * H, (h + 1) * H), v[...]))
        rs[...] = apply(split(gs[...]), ws[...], rs[...])

    run = jnp.where(z == 3, 0.0, rs[...])
    left = [jnp.concatenate([step[i][at(0), :] for step in steps], 0) for i in (0, 1)]
    all_z = mm(left, split(run[:N]))
    for i, (hi, lo, r) in enumerate(steps):
        zz = jnp.concatenate([all_z[i * B : (i + 1) * B], run[N:]], 0)
        out = r[...] + mm(split(zz), (hi[...], lo[...]), True)
        cov[2 - i] = out[:B]
        mean[2 - i : 3 - i] = out[B : B + 1]


def T(z, y, c):
    return (z % 4) * 8 + (y % 4) * 2 + c % 2


def tm_move(v, dz=0, dy=0, dc=0):
    perm = [(T(z + dz, y + dy, c + dc), T(z, y, c)) for z in range(4) for y in range(4) for c in range(2)]
    return lax.ppermute(v, "tm", perm)


def z_move(v, *pairs):
    perm = [(T(a, y, c), T(b, y, c)) for a, b in pairs for y in range(4) for c in range(2)]
    return lax.ppermute(v, "tm", perm)


def x_move(v, d):
    return lax.ppermute(v, "blk", [((i + d) % 4, i) for i in range(4)])


def swap(v):
    return tm_move(v, dc=1)


def after(first, *then):
    out = lax.optimization_barrier((first, then))
    return out[0], *out[1]


def local(filt_mean, filt_cov, pred_prec, transition):
    means = jnp.pad(filt_mean[:, None, :], ((0, 0), (0, 7), (0, 0)))
    full = (sds(N, N), sds(A, N))
    scratch = (pltpu.VMEM((N, N), F32), pltpu.VMEM((A, N), F32))
    keep = (sds(B + 8, N),)

    opposite, *sides = call(
        prep_kernel,
        (sds(3, RM, B),) + (sds(RM, N),) * 6,
        (filt_cov, pred_prec),
        (pltpu.VMEM((3, B, N), F32), pltpu.VMEM((3, B, N), F32), pltpu.SemaphoreType.DMA((6,))),
        name="prep",
        specs=[ANY, ANY],
        limit=60,
    )
    opposite = x_move(opposite, 2)
    send = lambda k: (x_move(sides[2 * k], 1), x_move(sides[2 * k + 1], -1))
    got = {2: send(2)}
    opposite, *sides[2:4] = after(opposite, *sides[2:4])
    got[1] = send(1)
    got[2], *sides[0:2] = after(got[2], *sides[0:2])
    got[0] = send(0)
    got = {k: (opposite, *got[k]) for k in got}
    half = jax.ShapeDtypeStruct((N, N), jnp.bfloat16)
    trans = call(
        split_kernel,
        (half, half),
        (transition,),
        (pltpu.VMEM((N, N), F32), pltpu.SemaphoreType.DMA),
        products=3,
        name="split",
        specs=[ANY],
    )
    args = {k: (filt_cov, pred_prec, got[k][1], got[k][2], got[k][0], *trans, means[k]) for k in got}
    back = (scratch[1], scratch[0])
    *run, keep2 = call(first_kernel, full + keep, args[2], back, products=3, name="first")
    g2 = run[0]
    *run, keep1 = call(second_kernel, full + keep, (*args[1], *run), back, products=5, name="second")
    g1 = run[0]
    g, n, g0, c = call(third_kernel, (full[0], full[1], full[0], full[1]), (*args[0], run[0]), scratch[:1], products=3, name="third")
    g_o = swap(g)
    r, keep0, packed = call(close_kernel, full[1:] + keep + (sds(2, RM, N),), (c, n, g0, run[1]), name="close")
    packed, g_o = after(packed, g_o)
    mg = call(pair_gain_kernel, sds(H, N), (g, g_o), name="pair_gain")
    up_g, down_g = tm_move(mg, dy=1), tm_move(mg, dy=-1)
    mr, r_o = call(pair_rest_kernel, (sds(RM, N), full[1]), (g, r, g_o, swap(packed)), name="pair_rest")
    up_r, down_r = tm_move(mr, dy=1), tm_move(mr, dy=-1)
    gains, rests = (g2, g1, g), (keep2, keep1, keep0)
    far = (tm_move(jnp.concatenate([up_g[:CUT], up_r], 0), dy=1), tm_move(down_g[CUT:], dy=-1))
    near = ()
    for pieces in ((mg, mr), (up_g, up_r), (down_g, down_r)):
        near += (*pieces, *map(swap, pieces))
    stacks = (sds(4, N, N), sds(4, A, N))
    maps = call(early_kernel, stacks, near, products=14, name="early")
    maps, *far = after(tuple(maps), *far)
    *maps, lr, hr, rm = call(
        late_kernel,
        stacks + (sds(A, N), sds(H + 8, N), sds(RM, N)),
        (*far, *map(swap, far), *maps),
        name="late",
        aliases={4: 0, 5: 1},
    )
    lg, *hg, gm = call(gain_kernel, (sds(N, N), half, half, sds(H, N)), maps[:1], name="gain")

    rm = z_move(rm, (3, 2), (1, 0))
    to_end = call(after_kernel, full, (lg, lr, *maps, g_o, r_o), scratch, name="after")
    to_end, gm = after(to_end, gm)
    to_end, rm = after(to_end, rm)
    gm = z_move(gm, (1, 0))
    rm_s = swap(rm)
    w = call(next_kernel, sds(RM, N), (*hg, hr, rm, rm_s), scratch[1:], name="next")
    w = z_move(w, (2, 1)) + z_move(w, (2, 0))
    folded = call(fold_kernel, (half, half, *keep) * 3, (*gains, *rests, *to_end), name="fold")
    folded, gm = after(folded, gm)
    folded, w = after(folded, w)
    smooth_cov, mean = call(
        final_kernel,
        (sds(3, B, N), sds(3, N)),
        (rm, rm_s, gm, swap(gm), w, swap(w), *folded),
        (scratch[1], scratch[0], scratch[1]),
        products=3.5,
        name="final",
    )
    return mean, smooth_cov


def solution(mesh):
    return jax.shard_map(
        local,
        mesh=mesh,
        in_specs=(P("tm", None), P("tm", "blk", None), P("tm", "blk", None), P()),
        out_specs=(P("tm", None), P("tm", "blk", None)),
        check_vma=False,
    )
```

```python
import functools

import jax
import jax.numpy as jnp
from jax import lax
from jax.experimental import pallas as pl
from jax.experimental.pallas import tpu as pltpu
from jax.sharding import PartitionSpec as P

N = 512
B = 128
H = 256
A = N + 8
F32 = jnp.float32
VM = pl.BlockSpec(memory_space=pltpu.VMEM)
ANY = pl.BlockSpec(memory_space=pl.ANY)
RM = B + 8
TALL = 4 * B + 8
CUT = 64


def split(v):
    hi = v.astype(jnp.bfloat16)
    return hi, (v - hi.astype(F32)).astype(jnp.bfloat16)


def dot(a, b, nt):
    return lax.dot_general(a, b, (((1,), (1 if nt else 0,)), ((), ())), preferred_element_type=F32)


def mm(a, b, nt=False):
    (ah, al), (bh, bl) = a, b
    return dot(ah, bh, nt) + (dot(ah, bl, nt) + dot(al, bh, nt))


def rows(s, lo, hi):
    return s[0][lo:hi], s[1][lo:hi]


def sds(*shape):
    return jax.ShapeDtypeStruct(shape, F32)


def call(body, outs, args, scratch=(), products=0.0, name=None, specs=None, limit=24, aliases=None):
    return pl.pallas_call(
        body,
        out_shape=outs,
        in_specs=specs or [VM] * len(args),
        out_specs=jax.tree.map(lambda _: VM, outs),
        scratch_shapes=list(scratch),
        input_output_aliases=aliases or {},
        compiler_params=pltpu.CompilerParams(vmem_limit_bytes=limit * 2**20),
        cost_estimate=pl.CostEstimate(flops=int(products * 6 * N**3) + 1000, bytes_accessed=1000, transcendentals=0),
        name=name,
    )(*args)


def place():
    t = lax.axis_index("tm")
    return t, t // 8, lax.rem(t // 2, 4), lax.rem(t, 2)


def blk(v, j):
    return v[:, j * B : (j + 1) * B]


def at(j):
    return pl.ds(pl.multiple_of(lax.rem(lax.axis_index("blk") + j, 4) * B, B), B)


def places():
    return lax.broadcasted_iota(jnp.int32, (B, B), 0), lax.broadcasted_iota(jnp.int32, (B, B), 1)


def pack(a, b):
    i, j = places()
    return jnp.where(i <= j, a, b), jnp.sum(jnp.where(i == j, b, 0.0), 0, keepdims=True)


def unpack(both, diagonal):
    i, j = places()
    turned = both.T
    return jnp.where(i <= j, both, turned), jnp.where(i > j, both, jnp.where(i < j, turned, diagonal))


def prep_kernel(cov, prec, opposite, *rest):
    sides, (c, p, sems) = rest[:6], rest[6:]
    copies = []
    for k in (2, 1, 0):
        for src, dst in ((cov, c), (prec, p)):
            copies.append(pltpu.make_async_copy(src.at[k], dst.at[k], sems.at[len(copies)]))
            copies[-1].start()
    for n, k in enumerate((2, 1, 0)):
        copies[2 * n].wait()
        copies[2 * n + 1].wait()
        x2, fr, fl = opposite.at[k], sides[2 * k], sides[2 * k + 1]
        packed, diagonal = pack(c[k, :, at(0)], p[k, :, at(0)])
        diagonal = jnp.broadcast_to(diagonal, (8, B))
        for out in (x2, fr, fl):
            out[0:B, :] = packed
        x2[B:RM, :] = diagonal
        for out, parts in ((fr, ((c, 1), (c, 2), (p, 1))), (fl, ((c, 3), (p, 2), (p, 3)))):
            out[N:TALL, :] = diagonal
            for i, (v, j) in enumerate(parts):
                out[(i + 1) * B : (i + 2) * B, :] = v[k, :, at(j)]


def split_kernel(t, hi, lo, v, sem):
    copy = pltpu.make_async_copy(t, v, sem)
    copy.start()
    copy.wait()
    hi[...], lo[...] = split(v[...])


def assemble(ref, k, own, known):
    ref[at(0), :] = own[k]
    for j in (1, 2, 3):
        ref[at(j), at(0)] = own[k, :, at(j)].T
    for (i, j), block in known.items():
        ref[at(i), at(j)] = block
        if i != j:
            ref[at(j), at(i)] = block.T


def open_step(k, c, p, fr, fl, x2, hi, lo, mean, cf, pf):
    x2 = x2.at[k]
    (c1, p1), (c2, p2), (c3, p3) = (unpack(v[0:B], v[n : n + 1]) for v, n in ((fr, N), (x2, B), (fl, N)))
    fr, fl = ([v[i * B : (i + 1) * B] for i in (1, 2, 3)] for v in (fr, fl))
    assemble(cf, k, c, {(1, 1): c1, (1, 2): fr[0], (1, 3): fr[1], (3, 3): c3, (3, 2): fl[0], (2, 2): c2})
    cf[N:A, :] = mean[...]
    assemble(pf, k, p, {(1, 1): p1, (1, 2): fr[2], (3, 3): p3, (3, 1): fl[1], (3, 2): fl[2], (2, 2): p2})
    n = mm(split(cf[...]), (hi[...], lo[...]), True)
    if k == 2:
        n = jnp.where(lax.axis_index("tm") == 31, 0.0, n)
    return n, mm(split(n[:N]), split(pf[...]))


def close_step(c, n, gs, ra, ro, keep):
    r = ra[...]
    z = jnp.concatenate([mm(gs, split(r[:N])), r[N:]], 0) - n
    ro[...] = c + mm(split(z), gs, True)
    keep[0:B] = ro[at(0), :]
    keep[B : B + 8] = ro[N:A]


def first_kernel(*refs):
    go, ro, keep, cf, pf = refs[8:]
    n, g = open_step(2, *refs[:8], cf, pf)
    go[...] = g
    ro[...] = cf[...] - mm(split(n), split(g), True)
    keep[0:B] = ro[at(0), :]
    keep[B : B + 8] = ro[N:A]


def second_kernel(*refs):
    ga, ra, go, ro, keep, cf, pf = refs[8:]
    n, g = open_step(1, *refs[:8], cf, pf)
    gs = split(g)
    go[...] = mm(gs, split(ga[...]))
    close_step(cf[...], n, gs, ra, ro, keep)


def third_kernel(*refs):
    ga, go, no, g0, cf, pf = refs[8:]
    n, g = open_step(0, *refs[:8], cf, pf)
    no[...] = n
    g0[...] = g
    go[...] = mm(split(g), split(ga[...]))


def close_kernel(c, n, g, ra, ro, keep, packed):
    close_step(c[...], n[...], split(g[...]), ra, ro, keep)
    for h in (0, 1):
        write_rest(h, rows_of(ro, h), packed.at[h])


def write_rest(h, r, m):
    if h == 0:
        packed, diagonal = pack(r[:B, :B], r[B:H, B:H])
        blocks = [packed] + [r[:B, j * B : (j + 1) * B] for j in (1, 2, 3)]
    else:
        packed, diagonal = pack(r[B:H, 3 * B : N], r[:B, H : 3 * B])
        blocks = [r[:B, B:H], r[B:H, B:H], r[B:H, H : 3 * B], packed]
    row = lax.broadcasted_iota(jnp.int32, (8, B), 0)
    if m.shape[-1] == B:
        last = jnp.where(row == 4, diagonal, 0.0)
        for j, block in enumerate(blocks):
            m[j * B : (j + 1) * B] = block
            last = jnp.where(row == j, r[H : H + 1, j * B : (j + 1) * B], last)
        m[N:TALL] = last
    else:
        for j, block in enumerate(blocks):
            m[0:B, j * B : (j + 1) * B] = block
        m[B:RM, 0:B] = jnp.where(row == 1, diagonal, r[H : H + 8, 0:B])
        m[B:RM, B:N] = r[H : H + 8, B:N]


def read_rest(h, m, r):
    tall = m.shape[-1] == B
    block = lambda j: m[j * B : (j + 1) * B] if tall else m[0:B, j * B : (j + 1) * B]
    diagonal = m[N + 4 : N + 5] if tall else m[B + 1 : B + 2, 0:B]
    if h == 0:
        r[0:B, 0:B], r[B:H, B:H] = unpack(block(0), diagonal)
        top = lax.broadcasted_iota(jnp.int32, (8, B), 0) == 0
        for j in range(4):
            mean = m[N + j : N + j + 1] if tall else m[B : B + 1, j * B : (j + 1) * B]
            r[N:A, j * B : (j + 1) * B] = jnp.where(top, mean, 0.0)
            if j:
                r[0:B, j * B : (j + 1) * B] = block(j)
                r[j * B : (j + 1) * B, 0:B] = block(j).T
    else:
        r[3 * B : N, 3 * B : N], r[H : 3 * B, H : 3 * B] = unpack(block(3), diagonal)
        r[3 * B : N, B:H] = block(1)
        r[3 * B : N, H : 3 * B] = block(2)
        r[H : 3 * B, B:H] = block(0)
        r[B:H, H : 3 * B] = block(0).T
        r[B:H, 3 * B : N] = block(1).T
        r[H : 3 * B, 3 * B : N] = block(2).T


def read_map(h, mg, mr, g, r):
    g[h * H : (h + 1) * H] = mg[...]
    read_rest(h, mr, r)


def both(core, own, other, read):
    for c in (0, 1):
        @pl.when(core == c)
        def _():
            read(c, *own)
            read(1 - c, *other)


def read_maps(core, own, other, g, r):
    both(core, own, other, lambda h, mg, mr: read_map(h, mg, mr, g, r))


def apply(gs, s, r):
    left, right = gs if isinstance(gs[0], tuple) else (gs, gs)
    z = jnp.concatenate([mm(left, split(s[:N])), s[N:]], 0)
    return r + mm(split(z), right, True)


def rows_of(ref, h):
    return jnp.concatenate([ref[h * H : (h + 1) * H], ref[N:A]], 0)


def pair_gain_kernel(g, go, mg):
    core = place()[3]

    def half(h, g0, g1):
        mg[...] = mm(split(g0[h * H : (h + 1) * H]), split(g1[...]))

    pl.when(core == 0)(lambda: half(0, g, go))
    pl.when(core == 1)(lambda: half(1, go, g))


def pair_rest_kernel(g, r, go, packed, mr, ro):
    core = place()[3]
    for h in (0, 1):
        read_rest(h, packed.at[h], ro)

    def half(h, g0, r0, r1):
        gs = split(g0[...])
        write_rest(h, apply((rows(gs, h * H, (h + 1) * H), gs), r1[...], rows_of(r0, h)), mr)

    pl.when(core == 0)(lambda: half(0, g, r, ro))
    pl.when(core == 1)(lambda: half(1, go, ro, r))


def compose(left, right, out):
    gs = split(left[0][...])
    out[0][...] = mm(gs, split(right[0][...]))
    out[1][...] = apply(gs, right[1][...], left[1][...])


def early_kernel(*refs):
    own, own_s, up, up_s, down, down_s, maps = [refs[2 * i : 2 * i + 2] for i in range(7)]
    _, _, y, core = place()
    slot = lambda i: (maps[0].at[i], maps[1].at[i])
    read_maps(core, own, own_s, *slot(3))
    read_maps(core, up, up_s, *slot(1))
    read_maps(core, down, down_s, *slot(2))
    even = lax.rem(y, 2) == 0
    compose(slot(jnp.where(even, 3, 2)), slot(jnp.where(even, 1, 3)), slot(0))


def order():
    y = place()[2]
    pick = lambda a, b, c, d: jnp.where(y == 0, a, jnp.where(y == 1, b, jnp.where(y == 2, c, d)))
    return pick(0, 0, 3, 1), pick(3, 1, 2, 3), pick(2, 3, 0, 0)


def late_kernel(*refs):
    far, far_s, (old_g, old_r, g, r, inner, own, rm) = refs[0:2], refs[2:4], refs[4:]
    core = place()[3]

    def read(h, upper, lower):
        g[3, h * H : h * H + CUT] = upper[0:CUT]
        g[3, h * H + CUT : (h + 1) * H] = lower[...]
        read_rest(h, upper.at[CUT : CUT + RM], r.at[3])

    both(core, far, far_s, read)
    first, second, third = order()
    inner[...] = apply(split(g[second]), r[third], r[second])
    gs = split(g[first])
    half = pl.ds(pl.multiple_of(core * H, H), H)
    add = jnp.concatenate([r[first, half, :], r[first, N:A, :]], 0)
    own[...] = apply((split(g[first, half, :]), gs), inner[...], add)
    for c in (0, 1):
        @pl.when(core == c)
        def _():
            write_rest(c, own[...], rm)


def gain_kernel(g, inner, hi, lo, gm):
    core = place()[3]
    first, second, third = order()
    inner[...] = mm(split(g[second]), split(g[third]))
    total = mm(split(g[first]), split(inner[...]))
    hi[...], lo[...] = split(total)
    for c in (0, 1):
        @pl.when(core == c)
        def _():
            gm[...] = total[c * H : (c + 1) * H]


def after_kernel(lg, lr, g, r, cg, cr, tg, tr, sg, sr):
    _, _, y, core = place()
    eg, er = g.at[1], r.at[1]

    def keep(g, r):
        sg[...] = g
        sr[...] = r

    @pl.when(y == 0)
    def _():
        compose((eg, er), (lg, lr), (sg, sr))

    pl.when(y == 1)(lambda: keep(lg[...], lr[...]))
    pl.when(y == 2)(lambda: keep(eg[...], er[...]))

    @pl.when(y == 3)
    def _():
        eye = lax.broadcasted_iota(jnp.int32, (N, N), 0) == lax.broadcasted_iota(jnp.int32, (N, N), 1)
        keep(eye.astype(F32), jnp.zeros((A, N), F32))

    pl.when(core == 0)(lambda: compose((cg, cr), (sg, sr), (tg, tr)))

    @pl.when(core == 1)
    def _():
        tg[...] = sg[...]
        tr[...] = sr[...]


def fold_kernel(ga, gb, gc, ra, rb, rc, tg, tr, m, m_s, *refs):
    out, rs = refs[:9], refs[9]
    _, z, _, core = place()
    ds, ts = split(tg[...]), split(tr[0:N])
    steps = [(g, r, *out[3 * i : 3 * i + 3]) for i, (g, r) in enumerate(((ga, ra), (gb, rb), (gc, rc)))]
    for g, r, hi, lo, s in steps:
        gs = split(g[...])
        hi[...], lo[...] = split(mm(gs, ds))
        z_rows = jnp.concatenate([mm(split(g[at(0), :]), ts), tr[N:A]], 0)
        s[...] = r[...] + mm(split(z_rows), gs, True)

    @pl.when(z == 0)
    def _():
        both(core, (m,), (m_s,), lambda h, v: read_rest(h, v, rs))
        ms = split(rs[0:N])
        for _, _, hi, lo, s in steps:
            z_rows = jnp.concatenate([mm((hi[at(0), :], lo[at(0), :]), ms), rs[N:A]], 0)
            s[...] += mm(split(z_rows), (hi[...], lo[...]), True)


def join_kernel(m, m_s, *refs):
    old, new, gs = refs[:6], refs[6:12], refs[12]
    _, z, _, core = place()

    @pl.when(z == 0)
    def _():
        both(core, (m,), (m_s,), lambda h, v: gs.__setitem__(slice(h * H, (h + 1) * H), v[...]))
        right = split(gs[...])
        for i in (0, 2, 4):
            new[i][...], new[i + 1][...] = split(mm((old[i][...], old[i + 1][...]), right))


def next_kernel(hi, lo, r, m, m_s, w, rs):
    _, z, _, core = place()

    @pl.when(z == 2)
    def _():
        both(core, (m,), (m_s,), lambda h, v: read_rest(h, v, rs))
        gs = hi[...], lo[...]
        for c in (0, 1):
            @pl.when(core == c)
            def _():
                write_rest(c, apply((rows(gs, c * H, (c + 1) * H), gs), rs[...], r[...]), w)

    @pl.when(z != 2)
    def _():
        w[...] = jnp.zeros((TALL, B), F32)


def final_kernel(m, m_s, w, w_s, *refs):
    steps, (cov, mean, rs) = [refs[3 * i : 3 * i + 3] for i in range(3)], refs[9:]
    _, z, _, core = place()

    @pl.when(z >= 2)
    def _():
        both(core, (m,), (m_s,), lambda h, v: read_rest(h, v, rs))

    @pl.when(z < 2)
    def _():
        both(core, (w,), (w_s,), lambda h, v: read_rest(h, v, rs))

    run = jnp.where(z == 3, 0.0, rs[...])
    left = [jnp.concatenate([step[i][at(0), :] for step in steps], 0) for i in (0, 1)]
    all_z = mm(left, split(run[:N]))
    for i, (hi, lo, r) in enumerate(steps):
        zz = jnp.concatenate([all_z[i * B : (i + 1) * B], run[N:]], 0)
        out = r[...] + mm(split(zz), (hi[...], lo[...]), True)
        cov[2 - i] = out[:B]
        mean[2 - i : 3 - i] = out[B : B + 1]


def T(z, y, c):
    return (z % 4) * 8 + (y % 4) * 2 + c % 2


def tm_move(v, dz=0, dy=0, dc=0):
    perm = [(T(z + dz, y + dy, c + dc), T(z, y, c)) for z in range(4) for y in range(4) for c in range(2)]
    return lax.ppermute(v, "tm", perm)


def z_move(v, *pairs):
    perm = [(T(a, y, c), T(b, y, c)) for a, b in pairs for y in range(4) for c in range(2)]
    return lax.ppermute(v, "tm", perm)


def x_move(v, d):
    return lax.ppermute(v, "blk", [((i + d) % 4, i) for i in range(4)])


def swap(v):
    return tm_move(v, dc=1)


def after(first, *then):
    out = lax.optimization_barrier((first, then))
    return out[0], *out[1]


def local(filt_mean, filt_cov, pred_prec, transition):
    means = jnp.pad(filt_mean[:, None, :], ((0, 0), (0, 7), (0, 0)))
    full = (sds(N, N), sds(A, N))
    scratch = (pltpu.VMEM((N, N), F32), pltpu.VMEM((A, N), F32))
    keep = (sds(B + 8, N),)

    opposite, *sides = call(
        prep_kernel,
        (sds(3, RM, B),) + (sds(TALL, B),) * 6,
        (filt_cov, pred_prec),
        (pltpu.VMEM((3, B, N), F32), pltpu.VMEM((3, B, N), F32), pltpu.SemaphoreType.DMA((6,))),
        name="prep",
        specs=[ANY, ANY],
        limit=60,
    )
    opposite = x_move(opposite, 2)
    send = lambda k: (x_move(sides[2 * k], 1), x_move(sides[2 * k + 1], -1))
    got = {2: send(2)}
    opposite, *sides[2:4] = after(opposite, *sides[2:4])
    got[1] = send(1)
    got[2], *sides[0:2] = after(got[2], *sides[0:2])
    got[0] = send(0)
    got = {k: (opposite, *got[k]) for k in got}
    half = jax.ShapeDtypeStruct((N, N), jnp.bfloat16)
    trans = call(
        split_kernel,
        (half, half),
        (transition,),
        (pltpu.VMEM((N, N), F32), pltpu.SemaphoreType.DMA),
        products=3,
        name="split",
        specs=[ANY],
    )
    args = {k: (filt_cov, pred_prec, got[k][1], got[k][2], got[k][0], *trans, means[k]) for k in got}
    back = (scratch[1], scratch[0])
    *run, keep2 = call(first_kernel, full + keep, args[2], back, products=3, name="first")
    g2 = run[0]
    *run, keep1 = call(second_kernel, full + keep, (*args[1], *run), back, products=5, name="second")
    g1 = run[0]
    g, n, g0, c = call(third_kernel, (full[0], full[1], full[0], full[1]), (*args[0], run[0]), scratch[:1], products=3, name="third")
    g_o = swap(g)
    r, keep0, packed = call(close_kernel, full[1:] + keep + (sds(2, RM, N),), (c, n, g0, run[1]), name="close")
    packed, g_o = after(packed, g_o)
    mg = call(pair_gain_kernel, sds(H, N), (g, g_o), name="pair_gain")
    up_g, down_g = tm_move(mg, dy=1), tm_move(mg, dy=-1)
    mr, r_o = call(pair_rest_kernel, (sds(RM, N), full[1]), (g, r, g_o, swap(packed)), name="pair_rest")
    up_r, down_r = tm_move(mr, dy=1), tm_move(mr, dy=-1)
    gains, rests = (g2, g1, g), (keep2, keep1, keep0)
    far = (tm_move(jnp.concatenate([up_g[:CUT], up_r], 0), dy=1), tm_move(down_g[CUT:], dy=-1))
    near = ()
    for pieces in ((mg, mr), (up_g, up_r), (down_g, down_r)):
        near += (*pieces, *map(swap, pieces))
    stacks = (sds(4, N, N), sds(4, A, N))
    maps = call(early_kernel, stacks, near, products=14, name="early")
    maps, *far = after(tuple(maps), *far)
    *maps, lr, hr, rm = call(
        late_kernel,
        stacks + (sds(A, N), sds(H + 8, N), sds(TALL, B)),
        (*far, *map(swap, far), *maps),
        name="late",
        aliases={4: 0, 5: 1},
    )
    lg, *hg, gm = call(gain_kernel, (sds(N, N), half, half, sds(H, N)), maps[:1], name="gain")

    rm = z_move(rm, (3, 2), (1, 0))
    to_end = call(after_kernel, full, (lg, lr, *maps, g_o, r_o), scratch, name="after")
    to_end, gm = after(to_end, gm)
    to_end, rm = after(to_end, rm)
    gm = z_move(gm, (1, 0))
    rm_s = swap(rm)
    w = call(next_kernel, sds(TALL, B), (*hg, hr, rm, rm_s), scratch[1:], name="next")
    w, *to_end = after(w, *to_end)
    w = z_move(w, (2, 1)) + z_move(w, (2, 0))
    folded = call(
        fold_kernel,
        (half, half, *keep) * 3,
        (*gains, *rests, *to_end, rm, rm_s),
        scratch[1:],
        name="fold",
    )
    folded, gm = after(tuple(folded), gm)
    joined = call(
        join_kernel,
        (half,) * 6,
        (gm, swap(gm), *(folded[3 * i + j] for i in range(3) for j in range(2))),
        scratch[:1],
        name="join",
        aliases={2 + i: i for i in range(6)},
    )
    steps = [v for i in range(3) for v in (*joined[2 * i : 2 * i + 2], folded[3 * i + 2])]
    smooth_cov, mean = call(
        final_kernel,
        (sds(3, B, N), sds(3, N)),
        (rm, rm_s, w, swap(w), *steps),
        scratch[1:],
        products=3.5,
        name="final",
    )
    return mean, smooth_cov


def solution(mesh):
    return jax.shard_map(
        local,
        mesh=mesh,
        in_specs=(P("tm", None), P("tm", "blk", None), P("tm", "blk", None), P()),
        out_specs=(P("tm", None), P("tm", "blk", None)),
        check_vma=False,
    )
```

```python
import functools

import jax
import jax.numpy as jnp
from jax import lax
from jax.experimental import pallas as pl
from jax.experimental.pallas import tpu as pltpu
from jax.sharding import PartitionSpec as P

N = 512
B = 128
H = 256
A = N + 8
F32 = jnp.float32
VM = pl.BlockSpec(memory_space=pltpu.VMEM)
ANY = pl.BlockSpec(memory_space=pl.ANY)
RM = B + 8
TALL = 4 * B + 8
CUT = 64


def split(v):
    hi = v.astype(jnp.bfloat16)
    return hi, (v - hi.astype(F32)).astype(jnp.bfloat16)


def dot(a, b, nt):
    return lax.dot_general(a, b, (((1,), (1 if nt else 0,)), ((), ())), preferred_element_type=F32)


def mm(a, b, nt=False):
    (ah, al), (bh, bl) = a, b
    return dot(ah, bh, nt) + (dot(ah, bl, nt) + dot(al, bh, nt))


def rows(s, lo, hi):
    return s[0][lo:hi], s[1][lo:hi]


def sds(*shape):
    return jax.ShapeDtypeStruct(shape, F32)


def call(body, outs, args, scratch=(), products=0.0, name=None, specs=None, limit=24, aliases=None):
    return pl.pallas_call(
        body,
        out_shape=outs,
        in_specs=specs or [VM] * len(args),
        out_specs=jax.tree.map(lambda _: VM, outs),
        scratch_shapes=list(scratch),
        input_output_aliases=aliases or {},
        compiler_params=pltpu.CompilerParams(vmem_limit_bytes=limit * 2**20),
        cost_estimate=pl.CostEstimate(flops=int(products * 6 * N**3) + 1000, bytes_accessed=1000, transcendentals=0),
        name=name,
    )(*args)


def place():
    t = lax.axis_index("tm")
    return t, t // 8, lax.rem(t // 2, 4), lax.rem(t, 2)


def blk(v, j):
    return v[:, j * B : (j + 1) * B]


def at(j):
    return pl.ds(pl.multiple_of(lax.rem(lax.axis_index("blk") + j, 4) * B, B), B)


def places():
    return lax.broadcasted_iota(jnp.int32, (B, B), 0), lax.broadcasted_iota(jnp.int32, (B, B), 1)


def pack(a, b):
    i, j = places()
    return jnp.where(i <= j, a, b), jnp.sum(jnp.where(i == j, b, 0.0), 0, keepdims=True)


def unpack(both, diagonal):
    i, j = places()
    turned = both.T
    return jnp.where(i <= j, both, turned), jnp.where(i > j, both, jnp.where(i < j, turned, diagonal))


def prep_kernel(cov, prec, opposite, *rest):
    sides, (c, p, sems) = rest[:6], rest[6:]
    copies = []
    for k in (2, 1, 0):
        for src, dst in ((cov, c), (prec, p)):
            copies.append(pltpu.make_async_copy(src.at[k], dst.at[k], sems.at[len(copies)]))
            copies[-1].start()
    lasts = jnp.zeros((8, B), F32)
    for n, k in enumerate((2, 1, 0)):
        copies[2 * n].wait()
        copies[2 * n + 1].wait()
        fr, fl = sides[2 * k], sides[2 * k + 1]
        packed, diagonal = pack(c[k, :, at(0)], p[k, :, at(0)])
        diagonal = jnp.broadcast_to(diagonal, (8, B))
        fr[0:B, :] = packed
        fl[0:B, :] = packed
        opposite[k * B : (k + 1) * B, :] = packed
        lasts = jnp.where(lax.broadcasted_iota(jnp.int32, (8, B), 0) == k, diagonal, lasts)
        for out, parts in ((fr, ((c, 1), (c, 2), (p, 1))), (fl, ((c, 3), (p, 2), (p, 3)))):
            out[N:TALL, :] = diagonal
            for i, (v, j) in enumerate(parts):
                out[(i + 1) * B : (i + 2) * B, :] = v[k, :, at(j)]
    opposite[3 * B : 3 * B + 8, :] = lasts


def split_kernel(t, hi, lo, v, sem):
    copy = pltpu.make_async_copy(t, v, sem)
    copy.start()
    copy.wait()
    hi[...], lo[...] = split(v[...])


def assemble(ref, k, own, known):
    ref[at(0), :] = own[k]
    for j in (1, 2, 3):
        ref[at(j), at(0)] = own[k, :, at(j)].T
    for (i, j), block in known.items():
        ref[at(i), at(j)] = block
        if i != j:
            ref[at(j), at(i)] = block.T


def open_step(k, c, p, fr, fl, x2, hi, lo, mean, cf, pf):
    (c1, p1), (c2, p2), (c3, p3) = (
        unpack(v[m : m + B], v[n : n + 1]) for v, m, n in ((fr, 0, N), (x2, k * B, 3 * B + k), (fl, 0, N))
    )
    fr, fl = ([v[i * B : (i + 1) * B] for i in (1, 2, 3)] for v in (fr, fl))
    assemble(cf, k, c, {(1, 1): c1, (1, 2): fr[0], (1, 3): fr[1], (3, 3): c3, (3, 2): fl[0], (2, 2): c2})
    cf[N:A, :] = mean[...]
    assemble(pf, k, p, {(1, 1): p1, (1, 2): fr[2], (3, 3): p3, (3, 1): fl[1], (3, 2): fl[2], (2, 2): p2})
    n = mm(split(cf[...]), (hi[...], lo[...]), True)
    if k == 2:
        n = jnp.where(lax.axis_index("tm") == 31, 0.0, n)
    return n, mm(split(n[:N]), split(pf[...]))


def close_step(c, n, gs, ra, ro, keep):
    r = ra[...]
    z = jnp.concatenate([mm(gs, split(r[:N])), r[N:]], 0) - n
    ro[...] = c + mm(split(z), gs, True)
    keep[0:B] = ro[at(0), :]
    keep[B : B + 8] = ro[N:A]


def first_kernel(*refs):
    go, ro, keep, cf, pf = refs[8:]
    n, g = open_step(2, *refs[:8], cf, pf)
    go[...] = g
    ro[...] = cf[...] - mm(split(n), split(g), True)
    keep[0:B] = ro[at(0), :]
    keep[B : B + 8] = ro[N:A]


def second_kernel(*refs):
    ga, ra, go, ro, keep, cf, pf = refs[8:]
    n, g = open_step(1, *refs[:8], cf, pf)
    gs = split(g)
    go[...] = mm(gs, split(ga[...]))
    close_step(cf[...], n, gs, ra, ro, keep)


def third_kernel(*refs):
    ga, go, no, g0, cf, pf = refs[8:]
    n, g = open_step(0, *refs[:8], cf, pf)
    no[...] = n
    g0[...] = g
    go[...] = mm(split(g), split(ga[...]))


def close_kernel(c, n, g, ra, ro, keep, packed):
    close_step(c[...], n[...], split(g[...]), ra, ro, keep)
    for h in (0, 1):
        write_rest(h, rows_of(ro, h), packed.at[h])


def write_rest(h, r, m):
    if h == 0:
        packed, diagonal = pack(r[:B, :B], r[B:H, B:H])
        blocks = [packed] + [r[:B, j * B : (j + 1) * B] for j in (1, 2, 3)]
    else:
        packed, diagonal = pack(r[B:H, 3 * B : N], r[:B, H : 3 * B])
        blocks = [r[:B, B:H], r[B:H, B:H], r[B:H, H : 3 * B], packed]
    row = lax.broadcasted_iota(jnp.int32, (8, B), 0)
    if m.shape[-1] == B:
        last = jnp.where(row == 4, diagonal, 0.0)
        for j, block in enumerate(blocks):
            m[j * B : (j + 1) * B] = block
            last = jnp.where(row == j, r[H : H + 1, j * B : (j + 1) * B], last)
        m[N:TALL] = last
    else:
        for j, block in enumerate(blocks):
            m[0:B, j * B : (j + 1) * B] = block
        m[B:RM, 0:B] = jnp.where(row == 1, diagonal, r[H : H + 8, 0:B])
        m[B:RM, B:N] = r[H : H + 8, B:N]


def read_rest(h, m, r):
    tall = m.shape[-1] == B
    block = lambda j: m[j * B : (j + 1) * B] if tall else m[0:B, j * B : (j + 1) * B]
    diagonal = m[N + 4 : N + 5] if tall else m[B + 1 : B + 2, 0:B]
    if h == 0:
        r[0:B, 0:B], r[B:H, B:H] = unpack(block(0), diagonal)
        top = lax.broadcasted_iota(jnp.int32, (8, B), 0) == 0
        for j in range(4):
            mean = m[N + j : N + j + 1] if tall else m[B : B + 1, j * B : (j + 1) * B]
            r[N:A, j * B : (j + 1) * B] = jnp.where(top, mean, 0.0)
            if j:
                r[0:B, j * B : (j + 1) * B] = block(j)
                r[j * B : (j + 1) * B, 0:B] = block(j).T
    else:
        r[3 * B : N, 3 * B : N], r[H : 3 * B, H : 3 * B] = unpack(block(3), diagonal)
        r[3 * B : N, B:H] = block(1)
        r[3 * B : N, H : 3 * B] = block(2)
        r[H : 3 * B, B:H] = block(0)
        r[B:H, H : 3 * B] = block(0).T
        r[B:H, 3 * B : N] = block(1).T
        r[H : 3 * B, 3 * B : N] = block(2).T


def read_map(h, mg, mr, g, r):
    g[h * H : (h + 1) * H] = mg[...]
    read_rest(h, mr, r)


def both(core, own, other, read):
    for c in (0, 1):
        @pl.when(core == c)
        def _():
            read(c, *own)
            read(1 - c, *other)


def read_maps(core, own, other, g, r):
    both(core, own, other, lambda h, mg, mr: read_map(h, mg, mr, g, r))


def apply(gs, s, r):
    left, right = gs if isinstance(gs[0], tuple) else (gs, gs)
    z = jnp.concatenate([mm(left, split(s[:N])), s[N:]], 0)
    return r + mm(split(z), right, True)


def rows_of(ref, h):
    return jnp.concatenate([ref[h * H : (h + 1) * H], ref[N:A]], 0)


def pair_gain_kernel(g, go, mg):
    core = place()[3]

    def half(h, g0, g1):
        mg[...] = mm(split(g0[h * H : (h + 1) * H]), split(g1[...]))

    pl.when(core == 0)(lambda: half(0, g, go))
    pl.when(core == 1)(lambda: half(1, go, g))


def pair_rest_kernel(g, r, go, packed, mr, ro):
    core = place()[3]
    for h in (0, 1):
        read_rest(h, packed.at[h], ro)

    def half(h, g0, r0, r1):
        gs = split(g0[...])
        write_rest(h, apply((rows(gs, h * H, (h + 1) * H), gs), r1[...], rows_of(r0, h)), mr)

    pl.when(core == 0)(lambda: half(0, g, r, ro))
    pl.when(core == 1)(lambda: half(1, go, ro, r))


def compose(left, right, out):
    gs = split(left[0][...])
    out[0][...] = mm(gs, split(right[0][...]))
    out[1][...] = apply(gs, right[1][...], left[1][...])


def early_kernel(*refs):
    own, own_s, up, up_s, down, down_s, maps = [refs[2 * i : 2 * i + 2] for i in range(7)]
    _, _, y, core = place()
    slot = lambda i: (maps[0].at[i], maps[1].at[i])
    read_maps(core, own, own_s, *slot(3))
    read_maps(core, up, up_s, *slot(1))
    read_maps(core, down, down_s, *slot(2))
    even = lax.rem(y, 2) == 0
    compose(slot(jnp.where(even, 3, 2)), slot(jnp.where(even, 1, 3)), slot(0))


def order():
    y = place()[2]
    pick = lambda a, b, c, d: jnp.where(y == 0, a, jnp.where(y == 1, b, jnp.where(y == 2, c, d)))
    return pick(0, 0, 3, 1), pick(3, 1, 2, 3), pick(2, 3, 0, 0)


def late_kernel(*refs):
    far, far_s, (old_g, old_r, g, r, inner, own, rm) = refs[0:2], refs[2:4], refs[4:]
    core = place()[3]

    def read(h, upper, lower):
        g[3, h * H : h * H + CUT] = upper[0:CUT]
        g[3, h * H + CUT : (h + 1) * H] = lower[...]
        read_rest(h, upper.at[CUT : CUT + RM], r.at[3])

    both(core, far, far_s, read)
    first, second, third = order()
    inner[...] = apply(split(g[second]), r[third], r[second])
    gs = split(g[first])
    half = pl.ds(pl.multiple_of(core * H, H), H)
    add = jnp.concatenate([r[first, half, :], r[first, N:A, :]], 0)
    own[...] = apply((split(g[first, half, :]), gs), inner[...], add)
    for c in (0, 1):
        @pl.when(core == c)
        def _():
            write_rest(c, own[...], rm)


def gain_kernel(g, inner, hi, lo, gm):
    core = place()[3]
    first, second, third = order()
    inner[...] = mm(split(g[second]), split(g[third]))
    total = mm(split(g[first]), split(inner[...]))
    hi[...], lo[...] = split(total)
    for c in (0, 1):
        @pl.when(core == c)
        def _():
            gm[...] = total[c * H : (c + 1) * H]


def after_kernel(lg, lr, g, r, cg, cr, tg, tr, sg, sr):
    _, _, y, core = place()
    eg, er = g.at[1], r.at[1]

    def keep(g, r):
        sg[...] = g
        sr[...] = r

    @pl.when(y == 0)
    def _():
        compose((eg, er), (lg, lr), (sg, sr))

    pl.when(y == 1)(lambda: keep(lg[...], lr[...]))
    pl.when(y == 2)(lambda: keep(eg[...], er[...]))

    @pl.when(y == 3)
    def _():
        eye = lax.broadcasted_iota(jnp.int32, (N, N), 0) == lax.broadcasted_iota(jnp.int32, (N, N), 1)
        keep(eye.astype(F32), jnp.zeros((A, N), F32))

    pl.when(core == 0)(lambda: compose((cg, cr), (sg, sr), (tg, tr)))

    @pl.when(core == 1)
    def _():
        tg[...] = sg[...]
        tr[...] = sr[...]


def fold_kernel(ga, gb, gc, ra, rb, rc, tg, tr, m, m_s, *refs):
    out, rs = refs[:9], refs[9]
    _, z, _, core = place()
    ds, ts = split(tg[...]), split(tr[0:N])
    steps = [(g, r, *out[3 * i : 3 * i + 3]) for i, (g, r) in enumerate(((ga, ra), (gb, rb), (gc, rc)))]
    for g, r, hi, lo, s in steps:
        gs = split(g[...])
        hi[...], lo[...] = split(mm(gs, ds))
        z_rows = jnp.concatenate([mm(split(g[at(0), :]), ts), tr[N:A]], 0)
        s[...] = r[...] + mm(split(z_rows), gs, True)

    @pl.when(z == 0)
    def _():
        both(core, (m,), (m_s,), lambda h, v: read_rest(h, v, rs))
        ms = split(rs[0:N])
        for _, _, hi, lo, s in steps:
            z_rows = jnp.concatenate([mm((hi[at(0), :], lo[at(0), :]), ms), rs[N:A]], 0)
            s[...] += mm(split(z_rows), (hi[...], lo[...]), True)


def join_kernel(m, m_s, *refs):
    old, new, gs = refs[:6], refs[6:12], refs[12]
    _, z, _, core = place()

    @pl.when(z == 0)
    def _():
        both(core, (m,), (m_s,), lambda h, v: gs.__setitem__(slice(h * H, (h + 1) * H), v[...]))
        right = split(gs[...])
        for i in (0, 2, 4):
            new[i][...], new[i + 1][...] = split(mm((old[i][...], old[i + 1][...]), right))


def next_kernel(hi, lo, r, m, m_s, w, rs):
    _, z, _, core = place()

    @pl.when(z == 2)
    def _():
        both(core, (m,), (m_s,), lambda h, v: read_rest(h, v, rs))
        gs = hi[...], lo[...]
        for c in (0, 1):
            @pl.when(core == c)
            def _():
                write_rest(c, apply((rows(gs, c * H, (c + 1) * H), gs), rs[...], r[...]), w)

    @pl.when(z != 2)
    def _():
        w[...] = jnp.zeros((TALL, B), F32)


def final_kernel(m, m_s, w, w_s, *refs):
    steps, (cov, mean, rs) = [refs[3 * i : 3 * i + 3] for i in range(3)], refs[9:]
    _, z, _, core = place()

    @pl.when(z >= 2)
    def _():
        both(core, (m,), (m_s,), lambda h, v: read_rest(h, v, rs))

    @pl.when(z < 2)
    def _():
        both(core, (w,), (w_s,), lambda h, v: read_rest(h, v, rs))

    run = jnp.where(z == 3, 0.0, rs[...])
    left = [jnp.concatenate([step[i][at(0), :] for step in steps], 0) for i in (0, 1)]
    all_z = mm(left, split(run[:N]))
    for i, (hi, lo, r) in enumerate(steps):
        zz = jnp.concatenate([all_z[i * B : (i + 1) * B], run[N:]], 0)
        out = r[...] + mm(split(zz), (hi[...], lo[...]), True)
        cov[2 - i] = out[:B]
        mean[2 - i : 3 - i] = out[B : B + 1]


def T(z, y, c):
    return (z % 4) * 8 + (y % 4) * 2 + c % 2


def tm_move(v, dz=0, dy=0, dc=0):
    perm = [(T(z + dz, y + dy, c + dc), T(z, y, c)) for z in range(4) for y in range(4) for c in range(2)]
    return lax.ppermute(v, "tm", perm)


def z_move(v, *pairs):
    perm = [(T(a, y, c), T(b, y, c)) for a, b in pairs for y in range(4) for c in range(2)]
    return lax.ppermute(v, "tm", perm)


def x_move(v, d):
    return lax.ppermute(v, "blk", [((i + d) % 4, i) for i in range(4)])


def swap(v):
    return tm_move(v, dc=1)


def after(first, *then):
    out = lax.optimization_barrier((first, then))
    return out[0], *out[1]


def local(filt_mean, filt_cov, pred_prec, transition):
    means = jnp.pad(filt_mean[:, None, :], ((0, 0), (0, 7), (0, 0)))
    full = (sds(N, N), sds(A, N))
    scratch = (pltpu.VMEM((N, N), F32), pltpu.VMEM((A, N), F32))
    keep = (sds(B + 8, N),)

    opposite, *sides = call(
        prep_kernel,
        (sds(3 * B + 8, B),) + (sds(TALL, B),) * 6,
        (filt_cov, pred_prec),
        (pltpu.VMEM((3, B, N), F32), pltpu.VMEM((3, B, N), F32), pltpu.SemaphoreType.DMA((6,))),
        name="prep",
        specs=[ANY, ANY],
        limit=60,
    )
    opposite = x_move(opposite, 2)
    send = lambda k: (x_move(sides[2 * k], 1), x_move(sides[2 * k + 1], -1))
    got = {2: send(2)}
    opposite, *sides[2:4] = after(opposite, *sides[2:4])
    got[1] = send(1)
    got[2], *sides[0:2] = after(got[2], *sides[0:2])
    got[0] = send(0)
    got = {k: (opposite, *got[k]) for k in got}
    half = jax.ShapeDtypeStruct((N, N), jnp.bfloat16)
    trans = call(
        split_kernel,
        (half, half),
        (transition,),
        (pltpu.VMEM((N, N), F32), pltpu.SemaphoreType.DMA),
        products=3,
        name="split",
        specs=[ANY],
    )
    args = {k: (filt_cov, pred_prec, got[k][1], got[k][2], got[k][0], *trans, means[k]) for k in got}
    back = (scratch[1], scratch[0])
    *run, keep2 = call(first_kernel, full + keep, args[2], back, products=3, name="first")
    g2 = run[0]
    *run, keep1 = call(second_kernel, full + keep, (*args[1], *run), back, products=5, name="second")
    g1 = run[0]
    g, n, g0, c = call(third_kernel, (full[0], full[1], full[0], full[1]), (*args[0], run[0]), scratch[:1], products=3, name="third")
    g_o = swap(g)
    r, keep0, packed = call(close_kernel, full[1:] + keep + (sds(2, RM, N),), (c, n, g0, run[1]), name="close")
    packed, g_o = after(packed, g_o)
    mg = call(pair_gain_kernel, sds(H, N), (g, g_o), name="pair_gain")
    up_g, down_g = tm_move(mg, dy=1), tm_move(mg, dy=-1)
    mr, r_o = call(pair_rest_kernel, (sds(RM, N), full[1]), (g, r, g_o, swap(packed)), name="pair_rest")
    up_r, down_r = tm_move(mr, dy=1), tm_move(mr, dy=-1)
    gains, rests = (g2, g1, g), (keep2, keep1, keep0)
    far = (tm_move(jnp.concatenate([up_g[:CUT], up_r], 0), dy=1), tm_move(down_g[CUT:], dy=-1))
    near = ()
    for pieces in ((mg, mr), (up_g, up_r), (down_g, down_r)):
        near += (*pieces, *map(swap, pieces))
    stacks = (sds(4, N, N), sds(4, A, N))
    maps = call(early_kernel, stacks, near, products=14, name="early")
    maps, *far = after(tuple(maps), *far)
    *maps, lr, hr, rm = call(
        late_kernel,
        stacks + (sds(A, N), sds(H + 8, N), sds(TALL, B)),
        (*far, *map(swap, far), *maps),
        name="late",
        aliases={4: 0, 5: 1},
    )
    lg, *hg, gm = call(gain_kernel, (sds(N, N), half, half, sds(H, N)), maps[:1], name="gain")

    rm = z_move(rm, (3, 2), (1, 0))
    to_end = call(after_kernel, full, (lg, lr, *maps, g_o, r_o), scratch, name="after")
    to_end, gm = after(to_end, gm)
    to_end, rm = after(to_end, rm)
    gm = z_move(gm, (1, 0))
    rm_s = swap(rm)
    w = call(next_kernel, sds(TALL, B), (*hg, hr, rm, rm_s), scratch[1:], name="next")
    w, *to_end = after(w, *to_end)
    w = z_move(w, (2, 1)) + z_move(w, (2, 0))
    folded = call(
        fold_kernel,
        (half, half, *keep) * 3,
        (*gains, *rests, *to_end, rm, rm_s),
        scratch[1:],
        name="fold",
    )
    folded, gm = after(tuple(folded), gm)
    joined = call(
        join_kernel,
        (half,) * 6,
        (gm, swap(gm), *(folded[3 * i + j] for i in range(3) for j in range(2))),
        scratch[:1],
        name="join",
        aliases={2 + i: i for i in range(6)},
    )
    steps = [v for i in range(3) for v in (*joined[2 * i : 2 * i + 2], folded[3 * i + 2])]
    smooth_cov, mean = call(
        final_kernel,
        (sds(3, B, N), sds(3, N)),
        (rm, rm_s, w, swap(w), *steps),
        scratch[1:],
        products=3.5,
        name="final",
    )
    return mean, smooth_cov


def solution(mesh):
    return jax.shard_map(
        local,
        mesh=mesh,
        in_specs=(P("tm", None), P("tm", "blk", None), P("tm", "blk", None), P()),
        out_specs=(P("tm", None), P("tm", "blk", None)),
        check_vma=False,
    )
```
